32 devices in a mesh: groups: 2 (over y), dp: 8 (over z, x), tp: 2 (over core).
Axes of the slice: x: 2, y: 2, z: 4, core: 2. Of those that a mesh axis runs over, the one named last changes fastest.
Arguments:
- cache_k: bfloat16 [256, 16, 512], P(('groups', 'dp'), None, 'tp'), parts along dimension 0, may hold values from -6 to 6
- cache_v: bfloat16 [256, 16, 512], P(('groups', 'dp'), None, 'tp'), parts along dimension 0, may hold values from -6 to 6
- sel_rows: int32 [256, 5], P('groups'), parts along dimension 0, may hold values from 0 to 15, as said below
- span_home: int32 [256], P('groups'), parts along dimension 0, may hold values from 0 to 127, as said below
- request_spans: int32 [80, 12], P(('groups', 'dp')), parts along dimension 0, may hold values from 0 to 127, as said below
- fresh_q: bfloat16 [80, 12, 5, 4096], P(('groups', 'dp'), None, None, 'tp'), parts along dimension 0, may hold values from -6 to 6
- fresh_k: bfloat16 [80, 12, 5, 512], P(('groups', 'dp'), None, None, 'tp'), parts along dimension 0, may hold values from -6 to 6
- fresh_v: bfloat16 [80, 12, 5, 512], P(('groups', 'dp'), None, None, 'tp'), parts along dimension 0, may hold values from -6 to 6
- question_q: bfloat16 [80, 32, 4096], P(('groups', 'dp'), None, 'tp'), parts along dimension 0, may hold values from -6 to 6
- question_k: bfloat16 [80, 32, 512], P(('groups', 'dp'), None, 'tp'), parts along dimension 0, may hold values from -6 to 6
- question_v: bfloat16 [80, 32, 512], P(('groups', 'dp'), None, 'tp'), parts along dimension 0, may hold values from -6 to 6
- question_len: int32 [80], P(('groups', 'dp')), parts along dimension 0, may hold values from 1 to 32
Outputs:
- recomputed: bfloat16 [80, 12, 5, 4096], P(('groups', 'dp'), None, None, 'tp'), parts along dimension 0
- answer: bfloat16 [80, 32, 4096], P(('groups', 'dp'), None, 'tp'), parts along dimension 0
The draws below stay inside these ranges and needn't reach their ends.
There are 2 independent parts, one for each index of `groups`. The reference program is written for one: setup_inputs(seed, part) draws one part's arguments, and reference() takes and returns one part's arrays. A program takes and returns all parts, laid end to end along the dimension named above; each array names one. Nothing has to cross between parts.
Inputs may be any that keep to these rules, and one draw needn't show every extreme that they name: `request_spans`: each index of dp holds 60 list entries; at most 8 of them name spans whose storage positions lie on one index of dp (position // 16), and some index reaches 8. `span_home`: A permutation of the positions. `sel_rows`: the rows of one position are distinct.
All inputs are finite; a program needn't handle non-finite values.
Results may differ from the reference program's by a relative error of at most 0.005.
Values may be sent and summed in bfloat16 or wider, within the bound.
No kernel may reach another device: no remote copies, remote signals or barrier semaphores. Data moves between devices by JAX's collectives and lax.ppermute only.
A program may use at most 64 MiB of HBM per device.

```python
import jax
import jax.numpy as jnp
from jax import lax

HEAD = 128
QH = 32
KVH = 4
LIST = 12
SEL = 5
SPAN = 16
REQ_DEV = 5
Q_MAX = 32
SPANS_DEV = 16
POOL = 128
REQUESTS = 40
N_DP = 8


def shared_layout(key):
    home = jax.random.permutation(jax.random.fold_in(key, 101), POOL).astype(jnp.int32)
    slot_count = LIST * REQ_DEV
    owner_keys = jax.random.split(jax.random.fold_in(key, 102), N_DP)
    orders = jax.vmap(lambda one_key: jax.random.permutation(one_key, N_DP))(owner_keys).astype(jnp.int32)
    owners = orders[:, jnp.arange(slot_count, dtype=jnp.int32) % N_DP]
    local = jax.random.randint(jax.random.fold_in(key, 103), (N_DP, slot_count), 0, SPANS_DEV).astype(jnp.int32)
    stored = owners * SPANS_DEV + local
    inverse = jnp.argsort(home, stable=True).astype(jnp.int32)
    return (home, inverse[stored].reshape(REQUESTS, LIST))


def drawn_field(key, shape):
    return jnp.clip(jax.random.normal(key, shape, jnp.float32), -6.0, 6.0)


def draw_span_home(key, part):
    layout = shared_layout(key)
    return layout[0]


def draw_request_spans(key, part):
    layout = shared_layout(key)
    return layout[1]


def draw_sel_rows(key, part):
    key = jax.random.fold_in(key, 7)
    row_keys = jax.random.split(key, POOL)
    picked = jax.vmap(lambda one_key: jax.random.permutation(one_key, SPAN)[:SEL])(row_keys)
    return picked.astype(jnp.int32)


def draw_question_len(key, part):
    key = jax.random.fold_in(key, 9)
    lengths = jax.random.randint(key, (REQUESTS,), 1, Q_MAX + 1).astype(jnp.int32)
    first = jnp.arange(REQUESTS, dtype=jnp.int32) == 0
    return jnp.where(first, Q_MAX, lengths).astype(jnp.int32)


def draw_cache_k(key, part):
    key = jax.random.fold_in(key, 31)
    shape = (POOL, SPAN, KVH * HEAD)
    field = drawn_field(key, shape)
    return field.astype(jnp.bfloat16)


def draw_fresh_q(key, part):
    key = jax.random.fold_in(key, 37)
    shape = (REQUESTS, LIST, SEL, QH * HEAD)
    field = drawn_field(key, shape)
    return field.astype(jnp.bfloat16)


def draw_question_q(key, part):
    key = jax.random.fold_in(key, 41)
    shape = (REQUESTS, Q_MAX, QH * HEAD)
    field = drawn_field(key, shape)
    return field.astype(jnp.bfloat16)


def shard_levels(own_key, extent, pieces, low, high):
    gain = 1.0
    for position, parts in pieces:
        draws = jax.random.uniform(jax.random.fold_in(jax.random.fold_in(own_key, 6), position), (parts,), jnp.float32, low / len(pieces), high / len(pieces))
        gain = gain * jnp.repeat(jnp.exp(draws), extent[position] // parts).reshape((-1,) + (1,) * (len(extent) - 1 - position))
    return gain


def normal_values(stream_key, dims, deviation, bound, shards=(), held_as=jnp.bfloat16):
    values = jax.random.normal(stream_key, dims, jnp.float32) * deviation
    if len(shards) > 0:
        values = shard_levels(stream_key, dims, shards, -0.22, 0.18) * values
    return jnp.clip(values, min=-bound, max=bound).astype(held_as)


def setup_inputs(seed: int = 0, part: int = 0) -> dict:
    splits = jax.random.split(jax.random.key(seed), 13)
    part_splits = jax.random.split(jax.random.fold_in(splits[12], part), 13)
    cache_k = draw_cache_k(jax.random.fold_in(jax.random.fold_in(splits[12], part), 71), part)
    cache_v = normal_values(part_splits[1], (POOL, SPAN, KVH * HEAD), 1.0, 6.0, ((0, 8), (2, 2)))
    sel_rows = draw_sel_rows(jax.random.fold_in(jax.random.fold_in(splits[12], part), 71), part)
    span_home = draw_span_home(jax.random.fold_in(jax.random.fold_in(splits[12], part), 71), part)
    request_spans = draw_request_spans(jax.random.fold_in(jax.random.fold_in(splits[12], part), 71), part)
    fresh_q = draw_fresh_q(jax.random.fold_in(jax.random.fold_in(splits[12], part), 71), part)
    fresh_k = normal_values(part_splits[6], (REQUESTS, LIST, SEL, KVH * HEAD), 1.0, 6.0, ((0, 8), (3, 2)))
    fresh_v = normal_values(part_splits[7], (REQUESTS, LIST, SEL, KVH * HEAD), 1.0, 6.0, ((0, 8), (3, 2)))
    question_q = draw_question_q(jax.random.fold_in(jax.random.fold_in(splits[12], part), 71), part)
    question_k = normal_values(part_splits[9], (REQUESTS, Q_MAX, KVH * HEAD), 1.0, 6.0, ((0, 8), (2, 2)))
    question_v = normal_values(part_splits[10], (REQUESTS, Q_MAX, KVH * HEAD), 1.0, 6.0, ((0, 8), (2, 2)))
    question_len = draw_question_len(jax.random.fold_in(jax.random.fold_in(splits[12], part), 71), part)
    return dict(cache_k=cache_k, cache_v=cache_v, sel_rows=sel_rows, span_home=span_home, request_spans=request_spans, fresh_q=fresh_q, fresh_k=fresh_k, fresh_v=fresh_v, question_q=question_q, question_k=question_k, question_v=question_v, question_len=question_len)


def math_sqrt(value):
    return float(value) ** 0.5

def attend(queries, keys, values, allowed):
    rows = queries.shape[0]
    width = keys.shape[0]
    kv_heads = keys.shape[1] // HEAD
    group = queries.shape[1] // keys.shape[1]
    q_heads = queries.astype(jnp.float32).reshape(rows, kv_heads, group, HEAD)
    k_heads = keys.astype(jnp.float32).reshape(width, kv_heads, HEAD)
    v_heads = values.astype(jnp.float32).reshape(width, kv_heads, HEAD)
    scores = jnp.einsum('nkgd,mkd->kgnm', q_heads, k_heads) * (1.0 / math_sqrt(HEAD))
    scores = jnp.where(allowed[None, None], scores, -1e+30)
    top = lax.optimization_barrier(jnp.max(scores, axis=-1, keepdims=True))
    exponent = jnp.exp(scores - top)
    weights = (exponent / lax.optimization_barrier(jnp.sum(exponent, axis=-1, keepdims=True))).astype(jnp.bfloat16)
    weights = lax.optimization_barrier(weights).astype(jnp.float32)
    result = jnp.einsum('kgnm,mkd->nkgd', weights, v_heads)
    return result.reshape(rows, kv_heads * group * HEAD)

def request_pass(f_query, b_keys, b_values, selected, q_query, q_keys, q_values, q_length):
    lists, picks = selected.shape
    span_len = b_keys.shape[0] // lists
    total = b_keys.shape[0]
    limit = (jnp.arange(lists, dtype=jnp.int32)[:, None] * span_len + selected).reshape(-1)
    allowed = jnp.arange(total, dtype=jnp.int32)[None, :] <= limit[:, None]
    redone = attend(f_query.reshape(lists * picks, -1), b_keys, b_values, allowed)
    redone = redone.astype(jnp.bfloat16).reshape(lists, picks, -1)
    q_rows = q_query.shape[0]
    keys = jnp.concatenate([b_keys, q_keys], axis=0)
    values = jnp.concatenate([b_values, q_values], axis=0)
    column = jnp.arange(total + q_rows, dtype=jnp.int32)[None, :]
    row = jnp.arange(q_rows, dtype=jnp.int32)[:, None]
    allowed_q = (column < total) | (column - total <= row)
    spoken = attend(q_query, keys, values, allowed_q)
    spoken = jnp.where(row < q_length, spoken, 0.0).astype(jnp.bfloat16)
    return (redone, spoken)

def reference(cache_k, cache_v, sel_rows, span_home, request_spans, fresh_q, fresh_k, fresh_v, question_q, question_k, question_v, question_len):
    positions = span_home[request_spans]

    def one_request(index):
        where_at = positions[index]
        selected = sel_rows[where_at]
        entry = jnp.arange(LIST, dtype=jnp.int32)[:, None]
        b_keys = cache_k[where_at].at[entry, selected].set(fresh_k[index])
        b_values = cache_v[where_at].at[entry, selected].set(fresh_v[index])
        b_keys = b_keys.reshape(LIST * SPAN, -1)
        b_values = b_values.reshape(LIST * SPAN, -1)
        return request_pass(fresh_q[index], b_keys, b_values, selected, question_q[index], question_k[index], question_v[index], question_len[index])
    redone, spoken = lax.map(one_request, jnp.arange(REQUESTS, dtype=jnp.int32))
    return (redone, spoken)
```

```python
import functools

import jax
import jax.numpy as jnp
from jax import lax
from jax.experimental import pallas as pl
from jax.experimental.pallas import tpu as pltpu
from jax.sharding import PartitionSpec as P

HEAD = 128
LANES = 128
ROW_TILE = 16
MASKED = -1e30
RING_MAX = 16
VMEM_LIMIT = 40 * 1024 * 1024


def fetch_pool(buffers, pool, sems):
    rows = buffers[0].shape[0]
    copies = [
        pltpu.make_async_copy(ref, pool.at[pl.ds(b * rows, rows)], sems.at[b])
        for b, ref in enumerate(buffers)
    ]
    for copy in copies:
        copy.start()
    for copy in copies:
        copy.wait()


def blend(limit, slots, pool, entry_rows, fresh_ref, question_ref, base, fresh_rows):
    lists, span_len = entry_rows
    picks = fresh_ref.shape[1]
    total = lists * span_len
    for j in range(lists):
        base[j * span_len : (j + 1) * span_len, :] = pool[slots(j)]
    fresh_rows[0:picks, 0:lists, :] = fresh_ref[0]
    q_rows = question_ref.shape[1]
    fresh_rows[picks : picks + q_rows // ROW_TILE] = question_ref[0].reshape(
        q_rows // ROW_TILE, ROW_TILE, -1
    )
    padded = base.shape[0]
    key = lax.broadcasted_iota(jnp.int32, (padded, LANES), 0)
    here = jnp.where(key == limit, 1.0, 0.0)
    placed = jnp.dot(
        here.astype(jnp.bfloat16),
        fresh_rows[...].reshape(LANES, -1),
        preferred_element_type=jnp.float32,
    )
    replaced = jnp.max(here, axis=1, keepdims=True) > 0.5
    del total
    return jnp.where(replaced, placed, base[...].astype(jnp.float32)).astype(jnp.bfloat16)


def clear(*refs):
    for ref in refs:
        ref[...] = jnp.zeros_like(ref)


def weights_kernel(n_buf, lists, span_len, slot_ref, limit_ref, fq_ref, qq_ref, fk_ref, qk_ref, *rest):
    buffers = rest[:n_buf]
    out_ref, pool, base, fresh_rows, queries, sems = rest[n_buf:]
    r = pl.program_id(0)
    kv_heads = out_ref.shape[1]
    rows_head = queries.shape[2] * ROW_TILE
    heads = queries.shape[1]
    picks = fq_ref.shape[1]

    @pl.when(r == 0)
    def _():
        clear(base, fresh_rows, queries)
        row = lax.broadcasted_iota(jnp.int32, (rows_head, LANES), 0)
        column = lax.broadcasted_iota(jnp.int32, (rows_head, LANES), 1)
        unit = jnp.where(row == column, 1.0, 0.0).astype(jnp.bfloat16)
        for g in range(kv_heads):
            for h in range(heads):
                queries[g, h, :, :, HEAD:] = unit.reshape(-1, ROW_TILE, LANES)
        fetch_pool(buffers, pool, sems)

    limit = limit_ref[0]
    keys = blend(
        limit,
        lambda j: slot_ref[r * lists + j],
        pool,
        (lists, span_len),
        fk_ref,
        qk_ref,
        base,
        fresh_rows,
    )
    key = lax.broadcasted_iota(jnp.int32, (keys.shape[0], LANES), 0)
    bias = jnp.where(key <= limit, 0.0, MASKED).astype(jnp.bfloat16)
    scale = 1.4426950408889634 / float(HEAD) ** 0.5
    for g in range(kv_heads):
        for h in range(heads):
            at = (g * heads + h) * HEAD
            queries[g, h, 0:picks, 0:lists, 0:HEAD] = fq_ref[0, :, :, at : at + HEAD]
            queries[g, h, picks:, :, 0:HEAD] = qq_ref[0, :, at : at + HEAD].reshape(-1, ROW_TILE, HEAD)
        table = jnp.concatenate([keys[:, g * HEAD : (g + 1) * HEAD], bias], axis=1)
        scores = lax.dot_general(
            queries[g].reshape(heads * rows_head, 2 * HEAD),
            table,
            (((1,), (1,)), ((), ())),
            preferred_element_type=jnp.float32,
        )
        top = jnp.max(scores, axis=1, keepdims=True)
        out_ref[0, g] = jnp.exp2((scores - top) * scale).astype(jnp.bfloat16)


def values_kernel(n_buf, lists, span_len, slot_ref, length_ref, limit_ref, w_ref, fv_ref, qv_ref, *rest):
    buffers = rest[:n_buf]
    redone_ref, spoken_ref, pool, base, fresh_rows, sems = rest[n_buf:]
    r = pl.program_id(0)
    kv_heads = w_ref.shape[1]
    picks = fv_ref.shape[1]
    q_rows = spoken_ref.shape[1]
    heads = spoken_ref.shape[2] // HEAD // kv_heads
    rows_head = picks * ROW_TILE + q_rows

    @pl.when(r == 0)
    def _():
        clear(base, fresh_rows)
        fetch_pool(buffers, pool, sems)

    values = blend(
        limit_ref[0],
        lambda j: slot_ref[r * lists + j],
        pool,
        (lists, span_len),
        fv_ref,
        qv_ref,
        base,
        fresh_rows,
    )
    ones = jnp.ones((values.shape[0], LANES), jnp.bfloat16)
    live = lax.broadcasted_iota(jnp.int32, (q_rows, HEAD), 0) < length_ref[r]
    for g in range(kv_heads):
        table = jnp.concatenate([values[:, g * HEAD : (g + 1) * HEAD], ones], axis=1)
        both = jnp.dot(w_ref[0, g], table, preferred_element_type=jnp.float32)
        result = both[:, :HEAD] / both[:, HEAD:]
        for h in range(heads):
            at = (g * heads + h) * HEAD
            row = h * rows_head
            fresh = result[row : row + picks * ROW_TILE].astype(jnp.bfloat16)
            redone_ref[0, :, :, at : at + HEAD] = fresh.reshape(picks, ROW_TILE, HEAD)[:, :lists, :]
            spoken = result[row + picks * ROW_TILE : row + rows_head]
            spoken_ref[0, :, at : at + HEAD] = jnp.where(live, spoken, 0.0).astype(jnp.bfloat16)


def attend(slots, limit, lengths, k_pieces, v_pieces, fresh_q, fresh_k, fresh_v, question_q, question_k, question_v):
    req_count, picks, lists, q_width = fresh_q.shape
    piece_rows, span_len, width = k_pieces[0].shape
    n_buf = len(k_pieces)
    q_rows = question_q.shape[1]
    kv_heads = width // HEAD
    heads = q_width // width
    rows_head = picks * ROW_TILE + q_rows
    padded = -(-(lists * span_len + q_rows) // LANES) * LANES

    def block(shape):
        return pl.BlockSpec((1,) + tuple(shape[1:]), lambda r, *_: (r,) + (0,) * (len(shape) - 1))

    anywhere = pl.BlockSpec(memory_space=pl.ANY)
    shared = [
        pltpu.VMEM((n_buf * piece_rows, span_len, width), jnp.bfloat16),
        pltpu.VMEM((padded, width), jnp.bfloat16),
        pltpu.VMEM((LANES // ROW_TILE, ROW_TILE, width), jnp.bfloat16),
    ]
    params = pltpu.CompilerParams(dimension_semantics=("arbitrary",), vmem_limit_bytes=VMEM_LIMIT)
    flops = 2 * req_count * kv_heads * heads * rows_head * padded * 2 * HEAD
    w_shape = (req_count, kv_heads, heads * rows_head, padded)
    weights = pl.pallas_call(
        functools.partial(weights_kernel, n_buf, lists, span_len),
        grid_spec=pltpu.PrefetchScalarGridSpec(
            num_scalar_prefetch=1,
            grid=(req_count,),
            in_specs=[
                block(limit.shape),
                block(fresh_q.shape),
                block(question_q.shape),
                block(fresh_k.shape),
                block(question_k.shape),
            ]
            + [anywhere] * n_buf,
            out_specs=block(w_shape),
            scratch_shapes=shared
            + [
                pltpu.VMEM((kv_heads, heads, rows_head // ROW_TILE, ROW_TILE, 2 * HEAD), jnp.bfloat16),
                pltpu.SemaphoreType.DMA((n_buf,)),
            ],
        ),
        out_shape=jax.ShapeDtypeStruct(w_shape, jnp.bfloat16),
        compiler_params=params,
        cost_estimate=pl.CostEstimate(flops=flops, bytes_accessed=8 << 20, transcendentals=flops // 512),
        name="span_weights",
    )(slots, limit, fresh_q, question_q, fresh_k, question_k, *k_pieces)
    return pl.pallas_call(
        functools.partial(values_kernel, n_buf, lists, span_len),
        grid_spec=pltpu.PrefetchScalarGridSpec(
            num_scalar_prefetch=2,
            grid=(req_count,),
            in_specs=[block(limit.shape), block(w_shape), block(fresh_v.shape), block(question_v.shape)]
            + [anywhere] * n_buf,
            out_specs=[block(fresh_q.shape), block(question_q.shape)],
            scratch_shapes=shared + [pltpu.SemaphoreType.DMA((n_buf,))],
        ),
        out_shape=[
            jax.ShapeDtypeStruct(fresh_q.shape, jnp.bfloat16),
            jax.ShapeDtypeStruct(question_q.shape, jnp.bfloat16),
        ],
        compiler_params=params,
        cost_estimate=pl.CostEstimate(flops=flops, bytes_accessed=8 << 20, transcendentals=0),
        name="span_values",
    )(slots, lengths, limit, weights, fresh_v, question_v, *v_pieces)


def ring_gather(keys, values, count):
    order = list(range(0, count, 2)) + list(range(1, count, 2))[::-1]
    onward = [(order[i], order[(i + 1) % count]) for i in range(count)]
    back = [(b, a) for a, b in onward]
    k_at, v_at = {0: keys}, {0: values}
    k_on = k_back = keys
    v_on = v_back = values
    half, rest = count // 2, (count - 1) // 2
    for hop in range(1, half + 1):
        k_on = lax.ppermute(k_on, "dp", onward)
        k_at[hop] = k_on
        if hop <= rest:
            k_back = lax.ppermute(k_back, "dp", back)
            k_at[count - hop] = k_back
            v_on = lax.ppermute(v_on, "dp", onward)
            v_at[hop] = v_on
        v_back = lax.ppermute(v_back, "dp", back)
        v_at[count - hop] = v_back
    return [k_at[d] for d in range(count)], [v_at[d] for d in range(count)]


def ring_slots(positions, spans_dev, count):
    def place(index):
        return jnp.where(index % 2 == 0, index // 2, count - 1 - index // 2)

    upstream = (place(lax.axis_index("dp")) - place(positions // spans_dev)) % count
    return upstream * spans_dev + positions % spans_dev


def asked_gather(keys, values, positions, spans_dev, count):
    slot_count = positions.shape[0]
    capacity = (slot_count + count - 1) // count
    owner = positions // spans_dev
    local = positions % spans_dev
    ids = jnp.arange(slot_count, dtype=jnp.int32)
    earlier = (owner[:, None] == owner[None, :]) & (ids[None, :] < ids[:, None])
    slots = owner * capacity + jnp.sum(earlier.astype(jnp.int32), axis=1)
    asking = jnp.full((count * capacity,), -1, jnp.int32).at[slots].set(local)
    wanted = jnp.maximum(lax.all_to_all(asking, "dp", split_axis=0, concat_axis=0, tiled=True), 0)
    pieces = [
        [lax.all_to_all(cache[wanted], "dp", split_axis=0, concat_axis=0, tiled=True)]
        for cache in (keys, values)
    ]
    return slots, pieces[0], pieces[1]


def shards(
    cache_k,
    cache_v,
    sel_rows,
    span_home,
    request_spans,
    fresh_q,
    fresh_k,
    fresh_v,
    question_q,
    question_k,
    question_v,
    question_len,
):
    count = lax.axis_size("dp")
    spans_dev, span_len, _ = cache_k.shape
    req_count, lists = request_spans.shape
    picks = sel_rows.shape[1]
    q_rows = question_q.shape[1]
    pool_ids = jnp.arange(span_home.shape[0], dtype=jnp.int32)
    positions = jnp.sum(
        jnp.where(request_spans[:, :, None] == pool_ids, span_home, 0), axis=-1, dtype=jnp.int32
    )
    selected = jnp.sum(
        jnp.where(positions[:, None, :, None] == pool_ids, sel_rows.T[None, :, None, :], 0),
        axis=-1,
        dtype=jnp.int32,
    )
    fresh_limit = jnp.arange(lists, dtype=jnp.int32) * span_len + selected
    fresh_limit = jnp.pad(fresh_limit, ((0, 0), (0, 0), (0, ROW_TILE - lists)), constant_values=-1)
    question_limit = lists * span_len + jnp.arange(q_rows, dtype=jnp.int32)
    limit = jnp.concatenate(
        [
            fresh_limit.reshape(req_count, picks * ROW_TILE),
            jnp.broadcast_to(question_limit, (req_count, q_rows)),
            jnp.full((req_count, LANES - picks * ROW_TILE - q_rows), -1, jnp.int32),
        ],
        axis=1,
    ).reshape(req_count, 1, LANES)
    flat = positions.reshape(-1)
    if count <= RING_MAX:
        slots = ring_slots(flat, spans_dev, count)
        k_pieces, v_pieces = ring_gather(cache_k, cache_v, count)
    else:
        slots, k_pieces, v_pieces = asked_gather(cache_k, cache_v, flat, spans_dev, count)
    turned = [jnp.transpose(a, (0, 2, 1, 3)) for a in (fresh_q, fresh_k, fresh_v)]
    redone, spoken = attend(
        slots, limit, question_len, k_pieces, v_pieces, *turned, question_q, question_k, question_v
    )
    return jnp.transpose(redone, (0, 2, 1, 3)), spoken


def solution(mesh):
    in_specs = (
        P(("groups", "dp"), None, "tp"),
        P(("groups", "dp"), None, "tp"),
        P("groups", None),
        P("groups"),
        P(("groups", "dp"), None),
        P(("groups", "dp"), None, None, "tp"),
        P(("groups", "dp"), None, None, "tp"),
        P(("groups", "dp"), None, None, "tp"),
        P(("groups", "dp"), None, "tp"),
        P(("groups", "dp"), None, "tp"),
        P(("groups", "dp"), None, "tp"),
        P(("groups", "dp")),
    )
    out_specs = (P(("groups", "dp"), None, None, "tp"), P(("groups", "dp"), None, "tp"))
    return jax.shard_map(shards, mesh=mesh, in_specs=in_specs, out_specs=out_specs, check_vma=False)
```

```python
import functools

import jax
import jax.numpy as jnp
from jax import lax
from jax.experimental import pallas as pl
from jax.experimental.pallas import tpu as pltpu
from jax.sharding import PartitionSpec as P

HEAD = 128
LANES = 128
ROW_TILE = 16
MASKED = -1e30
RING_MAX = 16
VMEM_LIMIT = 40 * 1024 * 1024


def clear(*refs):
    for ref in refs:
        ref[...] = jnp.zeros_like(ref)


def fill_pool(pieces, pool):
    rows = pieces[0].shape[0]
    for b, piece in enumerate(pieces):
        pool[b * rows : (b + 1) * rows] = piece[...]


def blend(limit, slots, pool, lists, fresh, question, base, fresh_rows):
    span_len = pool.shape[1]
    picks = fresh.shape[0]
    for j in range(lists):
        base[j * span_len : (j + 1) * span_len, :] = pool[slots(j)]
    fresh_rows[0:picks, 0:lists, :] = fresh
    q_tiles = question.shape[0] // ROW_TILE
    fresh_rows[picks : picks + q_tiles] = question.reshape(q_tiles, ROW_TILE, -1)
    key = lax.broadcasted_iota(jnp.int32, (base.shape[0], LANES), 0)
    here = jnp.where(key == limit, 1.0, 0.0)
    placed = jnp.dot(
        here.astype(jnp.bfloat16),
        fresh_rows[...].reshape(LANES, -1),
        preferred_element_type=jnp.float32,
    )
    replaced = jnp.max(here, axis=1, keepdims=True) > 0.5
    return jnp.where(replaced, placed, base[...].astype(jnp.float32)).astype(jnp.bfloat16)


def weights_kernel(n_buf, slot_ref, limit_ref, fq_hbm, qq_hbm, fk_hbm, qk_hbm, *rest):
    pieces = rest[:n_buf]
    out_ref, fq, qq, fk, qk, pool, base, fresh_rows, queries, sems = rest[n_buf:]
    req_count, picks, lists, _ = fq.shape
    kv_heads, heads = out_ref.shape[1], queries.shape[1]
    rows_head = queries.shape[2] * ROW_TILE
    small = [
        pltpu.make_async_copy(fk_hbm, fk, sems.at[0]),
        pltpu.make_async_copy(qk_hbm, qk, sems.at[1]),
    ]
    for copy in small:
        copy.start()

    def request_copies(r):
        return [
            pltpu.make_async_copy(fq_hbm.at[r], fq.at[r], sems.at[2 + 2 * r]),
            pltpu.make_async_copy(qq_hbm.at[r], qq.at[r], sems.at[3 + 2 * r]),
        ]

    for r in range(req_count):
        for copy in request_copies(r):
            copy.start()
    clear(base, fresh_rows, queries)
    row = lax.broadcasted_iota(jnp.int32, (rows_head, LANES), 0)
    column = lax.broadcasted_iota(jnp.int32, (rows_head, LANES), 1)
    unit = jnp.where(row == column, 1.0, 0.0).astype(jnp.bfloat16)
    for g in range(kv_heads):
        for h in range(heads):
            queries[g, h, :, :, HEAD:] = unit.reshape(-1, ROW_TILE, LANES)
    fill_pool(pieces, pool)
    for copy in small:
        copy.wait()
    scale = 1.4426950408889634 / float(HEAD) ** 0.5

    def request(r):
        for copy in request_copies(r):
            copy.wait()
        limit = limit_ref[r]
        keys = blend(
            limit, lambda j: slot_ref[r * lists + j], pool, lists, fk[r], qk[r], base, fresh_rows
        )
        key = lax.broadcasted_iota(jnp.int32, (keys.shape[0], LANES), 0)
        bias = jnp.where(key <= limit, 0.0, MASKED).astype(jnp.bfloat16)
        for g in range(kv_heads):
            for h in range(heads):
                at = (g * heads + h) * HEAD
                queries[g, h, 0:picks, 0:lists, 0:HEAD] = fq[r, :, :, at : at + HEAD]
                queries[g, h, picks:, :, 0:HEAD] = qq[r, :, at : at + HEAD].reshape(-1, ROW_TILE, HEAD)
            table = jnp.concatenate([keys[:, g * HEAD : (g + 1) * HEAD], bias], axis=1)
            scores = lax.dot_general(
                queries[g].reshape(heads * rows_head, 2 * HEAD),
                table,
                (((1,), (1,)), ((), ())),
                preferred_element_type=jnp.float32,
            )
            top = jnp.max(scores, axis=1, keepdims=True)
            out_ref[r, g] = jnp.exp2((scores - top) * scale).astype(jnp.bfloat16)

    for r in range(req_count):
        request(r)


def values_kernel(n_buf, slot_ref, length_ref, limit_ref, w_ref, fv_hbm, qv_hbm, *rest):
    pieces = rest[:n_buf]
    redone_hbm, spoken_hbm, fv, qv, redone, spoken, pool, base, fresh_rows, sems, out_sems = rest[n_buf:]
    req_count, picks, lists, _ = redone.shape
    kv_heads = w_ref.shape[1]
    q_rows = spoken.shape[1]
    heads = spoken.shape[2] // HEAD // kv_heads
    rows_head = picks * ROW_TILE + q_rows
    small = [
        pltpu.make_async_copy(fv_hbm, fv, sems.at[0]),
        pltpu.make_async_copy(qv_hbm, qv, sems.at[1]),
    ]
    for copy in small:
        copy.start()
    clear(base, fresh_rows)
    fill_pool(pieces, pool)
    for copy in small:
        copy.wait()

    def out_copies(r):
        return [
            pltpu.make_async_copy(redone.at[r], redone_hbm.at[r], out_sems.at[2 * r]),
            pltpu.make_async_copy(spoken.at[r], spoken_hbm.at[r], out_sems.at[2 * r + 1]),
        ]

    def request(r):
        values = blend(
            limit_ref[r],
            lambda j: slot_ref[r * lists + j],
            pool,
            lists,
            fv[r],
            qv[r],
            base,
            fresh_rows,
        )
        ones = jnp.ones((values.shape[0], LANES), jnp.bfloat16)
        live = lax.broadcasted_iota(jnp.int32, (q_rows, HEAD), 0) < length_ref[r]
        for g in range(kv_heads):
            table = jnp.concatenate([values[:, g * HEAD : (g + 1) * HEAD], ones], axis=1)
            both = jnp.dot(w_ref[r, g], table, preferred_element_type=jnp.float32)
            result = both[:, :HEAD] / both[:, HEAD:]
            for h in range(heads):
                at = (g * heads + h) * HEAD
                row = h * rows_head
                fresh = result[row : row + picks * ROW_TILE].astype(jnp.bfloat16)
                redone[r, :, :, at : at + HEAD] = fresh.reshape(picks, ROW_TILE, HEAD)[:, :lists, :]
                asked = result[row + picks * ROW_TILE : row + rows_head]
                spoken[r, :, at : at + HEAD] = jnp.where(live, asked, 0.0).astype(jnp.bfloat16)
        for copy in out_copies(r):
            copy.start()

    for r in range(req_count):
        request(r)
    for r in range(req_count):
        for copy in out_copies(r):
            copy.wait()


def attend(slots, limit, lengths, k_pieces, v_pieces, fresh_q, fresh_k, fresh_v, question_q, question_k, question_v):
    req_count, picks, lists, q_width = fresh_q.shape
    piece_rows, span_len, width = k_pieces[0].shape
    n_buf = len(k_pieces)
    q_rows = question_q.shape[1]
    kv_heads = width // HEAD
    heads = q_width // width
    rows_head = picks * ROW_TILE + q_rows
    padded = -(-(lists * span_len + q_rows) // LANES) * LANES

    smem = pl.BlockSpec(memory_space=pltpu.SMEM)
    vmem = pl.BlockSpec(memory_space=pltpu.VMEM)
    hbm = pl.BlockSpec(memory_space=pltpu.HBM)

    def in_vmem(x):
        return pltpu.with_memory_space_constraint(x, pltpu.VMEM)

    def in_hbm(x):
        return pltpu.with_memory_space_constraint(x, pltpu.HBM)

    def like(x):
        return pltpu.VMEM(x.shape, x.dtype)

    shared = [
        pltpu.VMEM((n_buf * piece_rows, span_len, width), jnp.bfloat16),
        pltpu.VMEM((padded, width), jnp.bfloat16),
        pltpu.VMEM((LANES // ROW_TILE, ROW_TILE, width), jnp.bfloat16),
    ]
    params = pltpu.CompilerParams(vmem_limit_bytes=VMEM_LIMIT)
    flops = 2 * req_count * kv_heads * heads * rows_head * padded * 2 * HEAD
    w_shape = (req_count, kv_heads, heads * rows_head, padded)
    weights = pl.pallas_call(
        functools.partial(weights_kernel, n_buf),
        in_specs=[smem, vmem] + [hbm] * 4 + [vmem] * n_buf,
        out_specs=vmem,
        scratch_shapes=[like(fresh_q), like(question_q), like(fresh_k), like(question_k)]
        + shared
        + [
            pltpu.VMEM((kv_heads, heads, rows_head // ROW_TILE, ROW_TILE, 2 * HEAD), jnp.bfloat16),
            pltpu.SemaphoreType.DMA((2 + 2 * req_count,)),
        ],
        out_shape=pltpu.VMEM(w_shape, jnp.bfloat16),
        compiler_params=params,
        cost_estimate=pl.CostEstimate(flops=flops, bytes_accessed=8 << 20, transcendentals=flops // 512),
        name="span_weights",
    )(slots, limit, *map(in_hbm, (fresh_q, question_q, fresh_k, question_k)), *map(in_vmem, k_pieces))
    return pl.pallas_call(
        functools.partial(values_kernel, n_buf),
        in_specs=[smem, smem, vmem, vmem] + [hbm] * 2 + [vmem] * n_buf,
        out_specs=[hbm, hbm],
        scratch_shapes=[like(fresh_v), like(question_v), like(fresh_q), like(question_q)]
        + shared
        + [pltpu.SemaphoreType.DMA((2,)), pltpu.SemaphoreType.DMA((2 * req_count,))],
        out_shape=[
            jax.ShapeDtypeStruct(fresh_q.shape, jnp.bfloat16),
            jax.ShapeDtypeStruct(question_q.shape, jnp.bfloat16),
        ],
        compiler_params=params,
        cost_estimate=pl.CostEstimate(flops=flops, bytes_accessed=8 << 20, transcendentals=0),
        name="span_values",
    )(slots, lengths, limit, in_vmem(weights), *map(in_hbm, (fresh_v, question_v)), *map(in_vmem, v_pieces))


def ring_gather(keys, values, count):
    order = list(range(0, count, 2)) + list(range(1, count, 2))[::-1]
    onward = [(order[i], order[(i + 1) % count]) for i in range(count)]
    back = [(b, a) for a, b in onward]
    k_at, v_at = {0: keys}, {0: values}
    k_on = k_back = keys
    v_on = v_back = values
    half, rest = count // 2, (count - 1) // 2
    for hop in range(1, half + 1):
        k_on = lax.ppermute(k_on, "dp", onward)
        k_at[hop] = k_on
        if hop <= rest:
            k_back = lax.ppermute(k_back, "dp", back)
            k_at[count - hop] = k_back
            v_on = lax.ppermute(v_on, "dp", onward)
            v_at[hop] = v_on
        v_back = lax.ppermute(v_back, "dp", back)
        v_at[count - hop] = v_back
    return [k_at[d] for d in range(count)], [v_at[d] for d in range(count)]


def ring_slots(positions, spans_dev, count):
    def place(index):
        return jnp.where(index % 2 == 0, index // 2, count - 1 - index // 2)

    upstream = (place(lax.axis_index("dp")) - place(positions // spans_dev)) % count
    return upstream * spans_dev + positions % spans_dev


def asked_gather(keys, values, positions, spans_dev, count):
    slot_count = positions.shape[0]
    capacity = (slot_count + count - 1) // count
    owner = positions // spans_dev
    local = positions % spans_dev
    ids = jnp.arange(slot_count, dtype=jnp.int32)
    earlier = (owner[:, None] == owner[None, :]) & (ids[None, :] < ids[:, None])
    slots = owner * capacity + jnp.sum(earlier.astype(jnp.int32), axis=1)
    asking = jnp.full((count * capacity,), -1, jnp.int32).at[slots].set(local)
    wanted = jnp.maximum(lax.all_to_all(asking, "dp", split_axis=0, concat_axis=0, tiled=True), 0)
    pieces = [
        [lax.all_to_all(cache[wanted], "dp", split_axis=0, concat_axis=0, tiled=True)]
        for cache in (keys, values)
    ]
    return slots, pieces[0], pieces[1]


def shards(
    cache_k,
    cache_v,
    sel_rows,
    span_home,
    request_spans,
    fresh_q,
    fresh_k,
    fresh_v,
    question_q,
    question_k,
    question_v,
    question_len,
):
    count = lax.axis_size("dp")
    spans_dev, span_len, _ = cache_k.shape
    req_count, lists = request_spans.shape
    picks = sel_rows.shape[1]
    q_rows = question_q.shape[1]
    pool_ids = jnp.arange(span_home.shape[0], dtype=jnp.int32)
    positions = jnp.sum(
        jnp.where(request_spans[:, :, None] == pool_ids, span_home, 0), axis=-1, dtype=jnp.int32
    )
    selected = jnp.sum(
        jnp.where(positions[:, None, :, None] == pool_ids, sel_rows.T[None, :, None, :], 0),
        axis=-1,
        dtype=jnp.int32,
    )
    fresh_limit = jnp.arange(lists, dtype=jnp.int32) * span_len + selected
    fresh_limit = jnp.pad(fresh_limit, ((0, 0), (0, 0), (0, ROW_TILE - lists)), constant_values=-1)
    question_limit = lists * span_len + jnp.arange(q_rows, dtype=jnp.int32)
    limit = jnp.concatenate(
        [
            fresh_limit.reshape(req_count, picks * ROW_TILE),
            jnp.broadcast_to(question_limit, (req_count, q_rows)),
            jnp.full((req_count, LANES - picks * ROW_TILE - q_rows), -1, jnp.int32),
        ],
        axis=1,
    ).reshape(req_count, 1, LANES)
    flat = positions.reshape(-1)
    if count <= RING_MAX:
        slots = ring_slots(flat, spans_dev, count)
        k_pieces, v_pieces = ring_gather(cache_k, cache_v, count)
    else:
        slots, k_pieces, v_pieces = asked_gather(cache_k, cache_v, flat, spans_dev, count)
    turned = [jnp.transpose(a, (0, 2, 1, 3)) for a in (fresh_q, fresh_k, fresh_v)]
    redone, spoken = attend(
        slots, limit, question_len, k_pieces, v_pieces, *turned, question_q, question_k, question_v
    )
    return jnp.transpose(redone, (0, 2, 1, 3)), spoken


def solution(mesh):
    in_specs = (
        P(("groups", "dp"), None, "tp"),
        P(("groups", "dp"), None, "tp"),
        P("groups", None),
        P("groups"),
        P(("groups", "dp"), None),
        P(("groups", "dp"), None, None, "tp"),
        P(("groups", "dp"), None, None, "tp"),
        P(("groups", "dp"), None, None, "tp"),
        P(("groups", "dp"), None, "tp"),
        P(("groups", "dp"), None, "tp"),
        P(("groups", "dp"), None, "tp"),
        P(("groups", "dp")),
    )
    out_specs = (P(("groups", "dp"), None, None, "tp"), P(("groups", "dp"), None, "tp"))
    return jax.shard_map(shards, mesh=mesh, in_specs=in_specs, out_specs=out_specs, check_vma=False)
```

```python
import functools

import jax
import jax.numpy as jnp
from jax import lax
from jax.experimental import pallas as pl
from jax.experimental.pallas import tpu as pltpu
from jax.sharding import PartitionSpec as P

HEAD = 128
LANES = 128
ROW_TILE = 16
MASKED = -1e30
RING_MAX = 16
VMEM_LIMIT = 40 * 1024 * 1024


def fill_pool(pieces, pool):
    rows = pieces[0].shape[0]
    for b, piece in enumerate(pieces):
        pool[b * rows : (b + 1) * rows] = piece[...]


def blend(first, slot_ref, pool, placed, keep, blended):
    span_len = pool.shape[1]
    total = keep.shape[0]
    for j in range(total // span_len):
        at = slice(j * span_len, (j + 1) * span_len)
        kept = jnp.concatenate([keep[at, :]] * (blended.shape[1] // LANES), axis=1)
        blended[at, :] = placed[at, :] + kept * pool[slot_ref[first + j]]
    blended[total:, :] = placed[total:, :]


def prepare_kernel(
    count, place_ref, *rest
):
    sources, rest = rest[:12], rest[12:]
    scalars, own_k, own_v, placed, keep, bias, queries, *rest = rest
    spans_ref, home_ref, sel_ref, length_ref, fk, fv, qk, qv, fq, qq, rows, limits, sems = rest
    req_count, picks, lists, width = fk.shape
    q_rows = qk.shape[1]
    spans_dev, span_len, _ = own_k.shape
    kv_heads, heads = queries.shape[1], queries.shape[2]
    total = lists * span_len
    copies = [
        pltpu.make_async_copy(source, target, sems.at[n])
        for n, (source, target) in enumerate(
            zip(
                sources,
                (spans_ref, home_ref, sel_ref, length_ref, fk, fv, qk, qv, fq, qq, own_k, own_v),
                strict=True,
            )
        )
    ]
    for copy in copies:
        copy.start()
    rows[...] = jnp.zeros_like(rows)
    queries[...] = jnp.zeros_like(queries)
    lane = lax.broadcasted_iota(jnp.int32, (1, LANES), 1)
    asked_at = lane - picks * ROW_TILE
    blank = jnp.where((asked_at >= 0) & (asked_at < q_rows), total + asked_at, -1)
    for copy in copies[:4]:
        copy.wait()
    for r in range(req_count):
        limit = blank
        for j in range(lists):
            position = home_ref[spans_ref[r, j]]
            owner = lax.div(position, spans_dev)
            half = lax.div(owner, 2)
            place = jnp.where(lax.rem(owner, 2) == 0, half, count - 1 - half)
            upstream = lax.rem(place_ref[0] - place + count, count)
            scalars[r * lists + j] = upstream * spans_dev + lax.rem(position, spans_dev)
            for i in range(picks):
                limit = jnp.where(lane == i * ROW_TILE + j, j * span_len + sel_ref[i, position], limit)
        limits[r] = limit
        scalars[req_count * lists + r] = length_ref[r]
    for copy in copies[4:8]:
        copy.wait()
    key = lax.broadcasted_iota(jnp.int32, (placed.shape[1], LANES), 0)
    for r in range(req_count):
        limit = limits[r]
        rows[0:picks, 0:lists, 0:width] = fk[r]
        rows[0:picks, 0:lists, width:] = fv[r]
        rows[picks : picks + q_rows // ROW_TILE, :, 0:width] = qk[r].reshape(-1, ROW_TILE, width)
        rows[picks : picks + q_rows // ROW_TILE, :, width:] = qv[r].reshape(-1, ROW_TILE, width)
        here = jnp.where(key == limit, 1.0, 0.0)
        placed[r] = jnp.dot(
            here.astype(jnp.bfloat16),
            rows[...].reshape(LANES, -1),
            preferred_element_type=jnp.float32,
        ).astype(jnp.bfloat16)
        taken = jnp.max(here[:total], axis=1, keepdims=True)
        keep[r] = jnp.broadcast_to(1.0 - taken, (total, LANES)).astype(jnp.bfloat16)
        bias[r] = jnp.where(key <= limit, 0.0, MASKED).astype(jnp.bfloat16)
    for copy in copies[8:]:
        copy.wait()
    for r in range(req_count):
        for g in range(kv_heads):
            for h in range(heads):
                at = (g * heads + h) * HEAD
                queries[r, g, h, 0:picks, 0:lists, :] = fq[r, :, :, at : at + HEAD]
                queries[r, g, h, picks:, :, :] = qq[r, :, at : at + HEAD].reshape(-1, ROW_TILE, HEAD)


def weights_kernel(n_buf, lists, slot_ref, placed, keep, bias, queries, *rest):
    pieces = rest[:n_buf]
    out_ref, pool, blended, units = rest[n_buf:]
    req_count, kv_heads, heads, tiles = queries.shape[:4]
    rows_head = tiles * ROW_TILE
    width = blended.shape[1]
    row = lax.broadcasted_iota(jnp.int32, (rows_head, LANES), 0)
    column = lax.broadcasted_iota(jnp.int32, (rows_head, LANES), 1)
    unit = jnp.where(row == column, 1.0, 0.0).astype(jnp.bfloat16)
    for h in range(heads):
        units[h * rows_head : (h + 1) * rows_head, :] = unit
    fill_pool(pieces, pool)
    scale = 1.4426950408889634 / float(HEAD) ** 0.5
    for r in range(req_count):
        blend(r * lists, slot_ref, pool, placed.at[r, :, 0:width], keep.at[r], blended)
        for g in range(kv_heads):
            table = jnp.concatenate([blended[:, g * HEAD : (g + 1) * HEAD], bias[r]], axis=1)
            stacked = queries[r, g].reshape(heads * rows_head, HEAD)
            scores = lax.dot_general(
                jnp.concatenate([stacked, units[...]], axis=1),
                table,
                (((1,), (1,)), ((), ())),
                preferred_element_type=jnp.float32,
            )
            top = jnp.max(scores, axis=1, keepdims=True)
            out_ref[r, g] = jnp.exp2((scores - top) * scale).astype(jnp.bfloat16)


def values_kernel(n_buf, slot_ref, w_ref, placed, keep, *rest):
    pieces = rest[:n_buf]
    redone_hbm, spoken_hbm, redone, spoken, pool, blended, out_sems = rest[n_buf:]
    req_count, picks, lists, _ = redone.shape
    kv_heads = w_ref.shape[1]
    q_rows = spoken.shape[1]
    heads = spoken.shape[2] // HEAD // kv_heads
    rows_head = picks * ROW_TILE + q_rows
    width = blended.shape[1]
    fill_pool(pieces, pool)

    def out_copies(r):
        return [
            pltpu.make_async_copy(redone.at[r], redone_hbm.at[r], out_sems.at[2 * r]),
            pltpu.make_async_copy(spoken.at[r], spoken_hbm.at[r], out_sems.at[2 * r + 1]),
        ]

    for r in range(req_count):
        blend(r * lists, slot_ref, pool, placed.at[r, :, width : 2 * width], keep.at[r], blended)
        ones = jnp.ones((blended.shape[0], LANES), jnp.bfloat16)
        length = slot_ref[req_count * lists + r]
        live = lax.broadcasted_iota(jnp.int32, (q_rows, HEAD), 0) < length
        for g in range(kv_heads):
            table = jnp.concatenate([blended[:, g * HEAD : (g + 1) * HEAD], ones], axis=1)
            both = jnp.dot(w_ref[r, g], table, preferred_element_type=jnp.float32)
            result = both[:, :HEAD] / both[:, HEAD:]
            for h in range(heads):
                at = (g * heads + h) * HEAD
                row = h * rows_head
                fresh = result[row : row + picks * ROW_TILE].astype(jnp.bfloat16)
                redone[r, :, :, at : at + HEAD] = fresh.reshape(picks, ROW_TILE, HEAD)[:, :lists, :]
                asked = result[row + picks * ROW_TILE : row + rows_head]
                spoken[r, :, at : at + HEAD] = jnp.where(live, asked, 0.0).astype(jnp.bfloat16)
        for copy in out_copies(r):
            copy.start()
    for r in range(req_count):
        for copy in out_copies(r):
            copy.wait()


SMEM_SPEC = pl.BlockSpec(memory_space=pltpu.SMEM)
VMEM_SPEC = pl.BlockSpec(memory_space=pltpu.VMEM)
HBM_SPEC = pl.BlockSpec(memory_space=pltpu.HBM)
PARAMS = pltpu.CompilerParams(vmem_limit_bytes=VMEM_LIMIT)


def in_vmem(x):
    return pltpu.with_memory_space_constraint(x, pltpu.VMEM)


def in_hbm(x):
    return pltpu.with_memory_space_constraint(x, pltpu.HBM)


def like(x):
    return pltpu.VMEM(x.shape, x.dtype)


def prepare(place, spans, home, sel, lengths, cache_k, cache_v, fresh_q, fresh_k, fresh_v, question_q, question_k, question_v):
    count = lax.axis_size("dp")
    req_count, picks, lists, q_width = fresh_q.shape
    _, span_len, width = cache_k.shape
    q_rows = question_q.shape[1]
    kv_heads, heads = width // HEAD, q_width // width
    total = lists * span_len
    padded = -(-(total + q_rows) // LANES) * LANES
    near = (spans, home, sel, lengths)
    held = (fresh_k, fresh_v, question_k, question_v, fresh_q, question_q)
    far = near + held + (cache_k, cache_v)
    bf16 = jnp.bfloat16
    return pl.pallas_call(
        functools.partial(prepare_kernel, count),
        in_specs=[SMEM_SPEC] + [HBM_SPEC] * len(far),
        out_specs=[SMEM_SPEC] + [VMEM_SPEC] * 6,
        out_shape=[
            pltpu.SMEM((req_count * lists + req_count,), jnp.int32),
            like(cache_k),
            like(cache_v),
            pltpu.VMEM((req_count, padded, 2 * width), bf16),
            pltpu.VMEM((req_count, total, LANES), bf16),
            pltpu.VMEM((req_count, padded, LANES), bf16),
            pltpu.VMEM((req_count, kv_heads, heads, picks + q_rows // ROW_TILE, ROW_TILE, HEAD), bf16),
        ],
        scratch_shapes=[pltpu.SMEM(x.shape, x.dtype) for x in near]
        + [like(x) for x in held]
        + [
            pltpu.VMEM((LANES // ROW_TILE, ROW_TILE, 2 * width), bf16),
            pltpu.VMEM((req_count, 1, LANES), jnp.int32),
            pltpu.SemaphoreType.DMA((len(far),)),
        ],
        compiler_params=PARAMS,
        cost_estimate=pl.CostEstimate(flops=0, bytes_accessed=8 << 20, transcendentals=0),
        name="span_prepare",
    )(place, *map(in_hbm, far))


def attend(scalars, placed, keep, bias, queries, k_pieces, v_pieces, redone_shape, spoken_shape):
    req_count, _, lists, _ = redone_shape
    piece_rows, span_len, width = k_pieces[0].shape
    n_buf = len(k_pieces)
    kv_heads, heads, tiles = queries.shape[1:4]
    padded = placed.shape[1]
    pool = pltpu.VMEM((n_buf * piece_rows, span_len, width), jnp.bfloat16)
    blended = pltpu.VMEM((padded, width), jnp.bfloat16)
    w_shape = (req_count, kv_heads, heads * tiles * ROW_TILE, padded)
    flops = 4 * req_count * kv_heads * heads * tiles * ROW_TILE * padded * HEAD
    weights = pl.pallas_call(
        functools.partial(weights_kernel, n_buf, lists),
        in_specs=[SMEM_SPEC] + [VMEM_SPEC] * (4 + n_buf),
        out_specs=VMEM_SPEC,
        scratch_shapes=[pool, blended, pltpu.VMEM((heads * tiles * ROW_TILE, LANES), jnp.bfloat16)],
        out_shape=pltpu.VMEM(w_shape, jnp.bfloat16),
        compiler_params=PARAMS,
        cost_estimate=pl.CostEstimate(flops=flops, bytes_accessed=8 << 20, transcendentals=flops // 512),
        name="span_weights",
    )(scalars, *map(in_vmem, (placed, keep, bias, queries)), *map(in_vmem, k_pieces))
    return pl.pallas_call(
        functools.partial(values_kernel, n_buf),
        in_specs=[SMEM_SPEC] + [VMEM_SPEC] * (3 + n_buf),
        out_specs=[HBM_SPEC, HBM_SPEC],
        scratch_shapes=[
            pltpu.VMEM(redone_shape, jnp.bfloat16),
            pltpu.VMEM(spoken_shape, jnp.bfloat16),
            pool,
            blended,
            pltpu.SemaphoreType.DMA((2 * req_count,)),
        ],
        out_shape=[
            jax.ShapeDtypeStruct(redone_shape, jnp.bfloat16),
            jax.ShapeDtypeStruct(spoken_shape, jnp.bfloat16),
        ],
        compiler_params=PARAMS,
        cost_estimate=pl.CostEstimate(flops=flops, bytes_accessed=8 << 20, transcendentals=0),
        name="span_values",
    )(scalars, *map(in_vmem, (weights, placed, keep)), *map(in_vmem, v_pieces))


def ring_gather(keys, values, count, ready):
    order = list(range(0, count, 2)) + list(range(1, count, 2))[::-1]
    onward = [(order[i], order[(i + 1) % count]) for i in range(count)]
    back = [(b, a) for a, b in onward]
    k_at, v_at = {0: keys}, {0: values}
    k_on = k_back = keys
    v_on = v_back = values
    half, rest = count // 2, (count - 1) // 2
    for hop in range(1, half + 1):
        k_on = lax.ppermute(k_on, "dp", onward)
        k_at[hop] = k_on
        if hop <= rest:
            k_back = lax.ppermute(k_back, "dp", back)
            k_at[count - hop] = k_back
            if hop == 1:
                k_back, _ = lax.optimization_barrier((k_back, ready))
            v_on = lax.ppermute(v_on, "dp", onward)
            v_at[hop] = v_on
        v_back = lax.ppermute(v_back, "dp", back)
        v_at[count - hop] = v_back
    return [k_at[d] for d in range(count)], [v_at[d] for d in range(count)]


def asked_gather(keys, values, positions, spans_dev, count):
    slot_count = positions.shape[0]
    capacity = (slot_count + count - 1) // count
    owner = positions // spans_dev
    local = positions % spans_dev
    ids = jnp.arange(slot_count, dtype=jnp.int32)
    earlier = (owner[:, None] == owner[None, :]) & (ids[None, :] < ids[:, None])
    slots = owner * capacity + jnp.sum(earlier.astype(jnp.int32), axis=1)
    asking = jnp.full((count * capacity,), -1, jnp.int32).at[slots].set(local)
    wanted = jnp.maximum(lax.all_to_all(asking, "dp", split_axis=0, concat_axis=0, tiled=True), 0)
    pieces = [
        [lax.all_to_all(cache[wanted], "dp", split_axis=0, concat_axis=0, tiled=True)]
        for cache in (keys, values)
    ]
    return slots, pieces[0], pieces[1]


def shards(
    cache_k,
    cache_v,
    sel_rows,
    span_home,
    request_spans,
    fresh_q,
    fresh_k,
    fresh_v,
    question_q,
    question_k,
    question_v,
    question_len,
):
    count = lax.axis_size("dp")
    spans_dev = cache_k.shape[0]
    turned_q, turned_k, turned_v = [jnp.transpose(x, (0, 2, 1, 3)) for x in (fresh_q, fresh_k, fresh_v)]
    me = lax.axis_index("dp")
    place = jnp.where(me % 2 == 0, me // 2, count - 1 - me // 2).astype(jnp.int32).reshape(1)
    scalars, own_k, own_v, placed, keep, bias, queries = prepare(
        place,
        request_spans,
        span_home,
        sel_rows.T,
        question_len,
        cache_k,
        cache_v,
        turned_q,
        turned_k,
        turned_v,
        question_q,
        question_k,
        question_v,
    )
    if count <= RING_MAX:
        k_pieces, v_pieces = ring_gather(cache_k, cache_v, count, own_k)
        k_pieces[0], v_pieces[0] = own_k, own_v
        scalars = pltpu.with_memory_space_constraint(scalars, pltpu.SMEM)
    else:
        pool_ids = jnp.arange(span_home.shape[0], dtype=jnp.int32)
        named = request_spans.reshape(-1, 1) == pool_ids
        positions = jnp.sum(jnp.where(named, span_home, 0), axis=-1, dtype=jnp.int32)
        slots, k_pieces, v_pieces = asked_gather(cache_k, cache_v, positions, spans_dev, count)
        scalars = jnp.concatenate([slots, question_len])
    redone, spoken = attend(
        scalars, placed, keep, bias, queries, k_pieces, v_pieces, turned_q.shape, question_q.shape
    )
    return jnp.transpose(redone, (0, 2, 1, 3)), spoken


def solution(mesh):
    in_specs = (
        P(("groups", "dp"), None, "tp"),
        P(("groups", "dp"), None, "tp"),
        P("groups", None),
        P("groups"),
        P(("groups", "dp"), None),
        P(("groups", "dp"), None, None, "tp"),
        P(("groups", "dp"), None, None, "tp"),
        P(("groups", "dp"), None, None, "tp"),
        P(("groups", "dp"), None, "tp"),
        P(("groups", "dp"), None, "tp"),
        P(("groups", "dp"), None, "tp"),
        P(("groups", "dp")),
    )
    out_specs = (P(("groups", "dp"), None, None, "tp"), P(("groups", "dp"), None, "tp"))
    return jax.shard_map(shards, mesh=mesh, in_specs=in_specs, out_specs=out_specs, check_vma=False)
```

```python
import functools

import jax
import jax.numpy as jnp
from jax import lax
from jax.experimental import pallas as pl
from jax.experimental.pallas import tpu as pltpu
from jax.sharding import PartitionSpec as P

HEAD = 128
LANES = 128
ROW_TILE = 16
MASKED = -1e30
RING_MAX = 16
VMEM_LIMIT = 40 * 1024 * 1024


def fill_pool(pieces, pool):
    row = 0
    for piece in pieces:
        pool[row : row + piece.shape[0]] = piece[...]
        row += piece.shape[0]


def blend(first, slot_ref, pool, placed, keep, blended):
    span_len = pool.shape[1]
    total = keep.shape[0]
    for j in range(total // span_len):
        at = slice(j * span_len, (j + 1) * span_len)
        kept = jnp.concatenate([keep[at, :]] * (blended.shape[1] // LANES), axis=1)
        blended[at, :] = placed[at, :] + kept * pool[slot_ref[first + j]]
    blended[total:, :] = placed[total:, :]


def prepare_kernel(
    count, place_ref, *rest
):
    sources, rest = rest[:12], rest[12:]
    scalars, own_k, own_v, placed, keep, bias, fq, qq, *rest = rest
    spans_ref, home_ref, sel_ref, length_ref, fk, fv, qk, qv, rows, limits, sems = rest
    req_count, picks, lists, width = fk.shape
    q_rows = qk.shape[1]
    spans_dev, span_len, _ = own_k.shape
    total = lists * span_len
    copies = [
        pltpu.make_async_copy(source, target, sems.at[n])
        for n, (source, target) in enumerate(
            zip(
                sources,
                (spans_ref, home_ref, sel_ref, length_ref, fk, fv, qk, qv, fq, qq, own_k, own_v),
                strict=True,
            )
        )
    ]
    for copy in copies:
        copy.start()
    rows[...] = jnp.zeros_like(rows)
    lane = lax.broadcasted_iota(jnp.int32, (1, LANES), 1)
    asked_at = lane - picks * ROW_TILE
    blank = jnp.where((asked_at >= 0) & (asked_at < q_rows), total + asked_at, -1)
    for copy in copies[:4]:
        copy.wait()
    for r in range(req_count):
        limit = blank
        for j in range(lists):
            position = home_ref[spans_ref[r, j]]
            owner = lax.div(position, spans_dev)
            half = lax.div(owner, 2)
            place = jnp.where(lax.rem(owner, 2) == 0, half, count - 1 - half)
            upstream = lax.rem(place_ref[0] - place + count, count)
            scalars[r * lists + j] = upstream * spans_dev + lax.rem(position, spans_dev)
            for i in range(picks):
                limit = jnp.where(lane == i * ROW_TILE + j, j * span_len + sel_ref[i, position], limit)
        limits[r] = limit
        scalars[req_count * lists + r] = length_ref[r]
    for copy in copies[4:8]:
        copy.wait()
    key = lax.broadcasted_iota(jnp.int32, (placed.shape[1], LANES), 0)
    for r in range(req_count):
        limit = limits[r]
        rows[0:picks, 0:lists, 0:width] = fk[r]
        rows[0:picks, 0:lists, width:] = fv[r]
        rows[picks : picks + q_rows // ROW_TILE, :, 0:width] = qk[r].reshape(-1, ROW_TILE, width)
        rows[picks : picks + q_rows // ROW_TILE, :, width:] = qv[r].reshape(-1, ROW_TILE, width)
        here = jnp.where(key == limit, 1.0, 0.0)
        placed[r] = jnp.dot(
            here.astype(jnp.bfloat16),
            rows[...].reshape(LANES, -1),
            preferred_element_type=jnp.float32,
        ).astype(jnp.bfloat16)
        taken = jnp.max(here[:total], axis=1, keepdims=True)
        keep[r] = jnp.broadcast_to(1.0 - taken, (total, LANES)).astype(jnp.bfloat16)
        bias[r] = jnp.where(key <= limit, 0.0, MASKED).astype(jnp.bfloat16)
    for copy in copies[8:]:
        copy.wait()


def weights_kernel(n_buf, slot_ref, placed, keep, bias, fq, qq, *rest):
    pieces = rest[:n_buf]
    out_ref, pool, blended, units, queries = rest[n_buf:]
    req_count, picks, lists, _ = fq.shape
    kv_heads, heads, tiles = queries.shape[:3]
    rows_head = tiles * ROW_TILE
    width = blended.shape[1]
    row = lax.broadcasted_iota(jnp.int32, (rows_head, LANES), 0)
    column = lax.broadcasted_iota(jnp.int32, (rows_head, LANES), 1)
    unit = jnp.where(row == column, 1.0, 0.0).astype(jnp.bfloat16)
    for h in range(heads):
        units[h * rows_head : (h + 1) * rows_head, :] = unit
    fill_pool(pieces, pool)
    scale = 1.4426950408889634 / float(HEAD) ** 0.5
    for r in range(req_count):
        blend(r * lists, slot_ref, pool, placed.at[r, :, 0:width], keep.at[r], blended)
        for g in range(kv_heads):
            table = jnp.concatenate([blended[:, g * HEAD : (g + 1) * HEAD], bias[r]], axis=1)
            for h in range(heads):
                at = (g * heads + h) * HEAD
                queries[g, h, 0:picks, 0:lists, :] = fq[r, :, :, at : at + HEAD]
                queries[g, h, picks:, :, :] = qq[r, :, at : at + HEAD].reshape(-1, ROW_TILE, HEAD)
            stacked = queries[g].reshape(heads * rows_head, HEAD)
            scores = lax.dot_general(
                jnp.concatenate([stacked, units[...]], axis=1),
                table,
                (((1,), (1,)), ((), ())),
                preferred_element_type=jnp.float32,
            )
            top = jnp.max(scores, axis=1, keepdims=True)
            out_ref[r, g] = jnp.exp2((scores - top) * scale).astype(jnp.bfloat16)


def values_kernel(n_buf, slot_ref, w_ref, placed, keep, *rest):
    pieces = rest[:n_buf]
    redone_hbm, spoken_hbm, redone, spoken, pool, blended, out_sems = rest[n_buf:]
    req_count, picks, lists, _ = redone.shape
    kv_heads = w_ref.shape[1]
    q_rows = spoken.shape[1]
    heads = spoken.shape[2] // HEAD // kv_heads
    rows_head = picks * ROW_TILE + q_rows
    width = blended.shape[1]
    fill_pool(pieces, pool)

    def out_copies(r):
        return [
            pltpu.make_async_copy(redone.at[r], redone_hbm.at[r], out_sems.at[2 * r]),
            pltpu.make_async_copy(spoken.at[r], spoken_hbm.at[r], out_sems.at[2 * r + 1]),
        ]

    for r in range(req_count):
        blend(r * lists, slot_ref, pool, placed.at[r, :, width : 2 * width], keep.at[r], blended)
        ones = jnp.ones((blended.shape[0], LANES), jnp.bfloat16)
        length = slot_ref[req_count * lists + r]
        live = lax.broadcasted_iota(jnp.int32, (q_rows, HEAD), 0) < length
        for g in range(kv_heads):
            table = jnp.concatenate([blended[:, g * HEAD : (g + 1) * HEAD], ones], axis=1)
            both = jnp.dot(w_ref[r, g], table, preferred_element_type=jnp.float32)
            result = both[:, :HEAD] / both[:, HEAD:]
            for h in range(heads):
                at = (g * heads + h) * HEAD
                row = h * rows_head
                fresh = result[row : row + picks * ROW_TILE].astype(jnp.bfloat16)
                redone[r, :, :, at : at + HEAD] = fresh.reshape(picks, ROW_TILE, HEAD)[:, :lists, :]
                asked = result[row + picks * ROW_TILE : row + rows_head]
                spoken[r, :, at : at + HEAD] = jnp.where(live, asked, 0.0).astype(jnp.bfloat16)
        for copy in out_copies(r):
            copy.start()
    for r in range(req_count):
        for copy in out_copies(r):
            copy.wait()


SMEM_SPEC = pl.BlockSpec(memory_space=pltpu.SMEM)
VMEM_SPEC = pl.BlockSpec(memory_space=pltpu.VMEM)
HBM_SPEC = pl.BlockSpec(memory_space=pltpu.HBM)
PARAMS = pltpu.CompilerParams(vmem_limit_bytes=VMEM_LIMIT)


def in_vmem(x):
    return pltpu.with_memory_space_constraint(x, pltpu.VMEM)


def in_hbm(x):
    return pltpu.with_memory_space_constraint(x, pltpu.HBM)


def like(x):
    return pltpu.VMEM(x.shape, x.dtype)


def prepare(place, spans, home, sel, lengths, cache_k, cache_v, fresh_q, fresh_k, fresh_v, question_q, question_k, question_v):
    count = lax.axis_size("dp")
    req_count, picks, lists, _ = fresh_q.shape
    _, span_len, width = cache_k.shape
    q_rows = question_q.shape[1]
    total = lists * span_len
    padded = -(-(total + q_rows) // LANES) * LANES
    near = (spans, home, sel, lengths)
    held = (fresh_k, fresh_v, question_k, question_v)
    far = near + held + (fresh_q, question_q, cache_k, cache_v)
    bf16 = jnp.bfloat16
    return pl.pallas_call(
        functools.partial(prepare_kernel, count),
        in_specs=[SMEM_SPEC] + [HBM_SPEC] * len(far),
        out_specs=[SMEM_SPEC] + [VMEM_SPEC] * 7,
        out_shape=[
            pltpu.SMEM((req_count * lists + req_count,), jnp.int32),
            like(cache_k),
            like(cache_v),
            pltpu.VMEM((req_count, padded, 2 * width), bf16),
            pltpu.VMEM((req_count, total, LANES), bf16),
            pltpu.VMEM((req_count, padded, LANES), bf16),
            like(fresh_q),
            like(question_q),
        ],
        scratch_shapes=[pltpu.SMEM(x.shape, x.dtype) for x in near]
        + [like(x) for x in held]
        + [
            pltpu.VMEM((LANES // ROW_TILE, ROW_TILE, 2 * width), bf16),
            pltpu.VMEM((req_count, 1, LANES), jnp.int32),
            pltpu.SemaphoreType.DMA((len(far),)),
        ],
        compiler_params=PARAMS,
        cost_estimate=pl.CostEstimate(flops=0, bytes_accessed=8 << 20, transcendentals=0),
        name="span_prepare",
    )(place, *map(in_hbm, far))


def attend(scalars, placed, keep, bias, fresh_q, question_q, k_pieces, v_pieces):
    req_count, picks, _, q_width = fresh_q.shape
    _, span_len, width = k_pieces[0].shape
    n_buf = len(k_pieces)
    kv_heads, heads = width // HEAD, q_width // width
    tiles = picks + question_q.shape[1] // ROW_TILE
    padded = placed.shape[1]
    pool = pltpu.VMEM((sum(x.shape[0] for x in k_pieces), span_len, width), jnp.bfloat16)
    blended = pltpu.VMEM((padded, width), jnp.bfloat16)
    w_shape = (req_count, kv_heads, heads * tiles * ROW_TILE, padded)
    flops = 4 * req_count * kv_heads * heads * tiles * ROW_TILE * padded * HEAD
    weights = pl.pallas_call(
        functools.partial(weights_kernel, n_buf),
        in_specs=[SMEM_SPEC] + [VMEM_SPEC] * (5 + n_buf),
        out_specs=VMEM_SPEC,
        scratch_shapes=[pool, blended, pltpu.VMEM((heads * tiles * ROW_TILE, LANES), jnp.bfloat16)]
        + [pltpu.VMEM((kv_heads, heads, tiles, ROW_TILE, HEAD), jnp.bfloat16)],
        out_shape=pltpu.VMEM(w_shape, jnp.bfloat16),
        compiler_params=PARAMS,
        cost_estimate=pl.CostEstimate(flops=flops, bytes_accessed=8 << 20, transcendentals=flops // 512),
        name="span_weights",
    )(scalars, *map(in_vmem, (placed, keep, bias, fresh_q, question_q)), *map(in_vmem, k_pieces))
    n_buf = len(v_pieces)
    return pl.pallas_call(
        functools.partial(values_kernel, n_buf),
        in_specs=[SMEM_SPEC] + [VMEM_SPEC] * (3 + n_buf),
        out_specs=[HBM_SPEC, HBM_SPEC],
        scratch_shapes=[
            like(fresh_q),
            like(question_q),
            pool,
            blended,
            pltpu.SemaphoreType.DMA((2 * req_count,)),
        ],
        out_shape=[
            jax.ShapeDtypeStruct(fresh_q.shape, jnp.bfloat16),
            jax.ShapeDtypeStruct(question_q.shape, jnp.bfloat16),
        ],
        compiler_params=PARAMS,
        cost_estimate=pl.CostEstimate(flops=flops, bytes_accessed=8 << 20, transcendentals=0),
        name="span_values",
    )(scalars, *map(in_vmem, (weights, placed, keep)), *map(in_vmem, v_pieces))


def ring_gather(keys, values, count, ready):
    order = list(range(0, count, 2)) + list(range(1, count, 2))[::-1]
    onward = [(order[i], order[(i + 1) % count]) for i in range(count)]
    back = [(b, a) for a, b in onward]
    half, rest = count // 2, (count - 1) // 2
    cut = keys.shape[0] // 2
    k_at, v_at = {0: [keys]}, {0: [values]}
    k_on = k_back = keys
    v_on = v_back = values
    for hop in range(1, rest + 1):
        k_on = lax.ppermute(k_on, "dp", onward)
        k_at[hop] = [k_on]
        k_back = lax.ppermute(k_back, "dp", back)
        k_at[count - hop] = [k_back]
        if hop == 1:
            k_back, _ = lax.optimization_barrier((k_back, ready))
        v_on = lax.ppermute(v_on, "dp", onward)
        v_at[hop] = [v_on]
        v_back = lax.ppermute(v_back, "dp", back)
        v_at[count - hop] = [v_back]
    if half > rest:
        k_at[half] = [lax.ppermute(k_on, "dp", onward)]
        v_at[half] = [lax.ppermute(v_back, "dp", back)]
    gathered = []
    for at in (k_at, v_at):
        gathered.append([piece for d in range(count) for piece in at[d]])
    return gathered


def asked_gather(keys, values, positions, spans_dev, count):
    slot_count = positions.shape[0]
    capacity = (slot_count + count - 1) // count
    owner = positions // spans_dev
    local = positions % spans_dev
    ids = jnp.arange(slot_count, dtype=jnp.int32)
    earlier = (owner[:, None] == owner[None, :]) & (ids[None, :] < ids[:, None])
    slots = owner * capacity + jnp.sum(earlier.astype(jnp.int32), axis=1)
    asking = jnp.full((count * capacity,), -1, jnp.int32).at[slots].set(local)
    wanted = jnp.maximum(lax.all_to_all(asking, "dp", split_axis=0, concat_axis=0, tiled=True), 0)
    pieces = [
        [lax.all_to_all(cache[wanted], "dp", split_axis=0, concat_axis=0, tiled=True)]
        for cache in (keys, values)
    ]
    return slots, pieces[0], pieces[1]


def shards(
    cache_k,
    cache_v,
    sel_rows,
    span_home,
    request_spans,
    fresh_q,
    fresh_k,
    fresh_v,
    question_q,
    question_k,
    question_v,
    question_len,
):
    count = lax.axis_size("dp")
    spans_dev = cache_k.shape[0]
    turned_q, turned_k, turned_v = [jnp.transpose(x, (0, 2, 1, 3)) for x in (fresh_q, fresh_k, fresh_v)]
    me = lax.axis_index("dp")
    place = jnp.where(me % 2 == 0, me // 2, count - 1 - me // 2).astype(jnp.int32).reshape(1)
    scalars, own_k, own_v, placed, keep, bias, held_q, asked_q = prepare(
        place,
        request_spans,
        span_home,
        sel_rows.T,
        question_len,
        cache_k,
        cache_v,
        turned_q,
        turned_k,
        turned_v,
        question_q,
        question_k,
        question_v,
    )
    if count <= RING_MAX:
        k_pieces, v_pieces = ring_gather(cache_k, cache_v, count, own_k)
        k_pieces[0], v_pieces[0] = own_k, own_v
        scalars = pltpu.with_memory_space_constraint(scalars, pltpu.SMEM)
    else:
        pool_ids = jnp.arange(span_home.shape[0], dtype=jnp.int32)
        named = request_spans.reshape(-1, 1) == pool_ids
        positions = jnp.sum(jnp.where(named, span_home, 0), axis=-1, dtype=jnp.int32)
        slots, k_pieces, v_pieces = asked_gather(cache_k, cache_v, positions, spans_dev, count)
        scalars = jnp.concatenate([slots, question_len])
    redone, spoken = attend(
        scalars, placed, keep, bias, held_q, asked_q, k_pieces, v_pieces
    )
    return jnp.transpose(redone, (0, 2, 1, 3)), spoken


def solution(mesh):
    in_specs = (
        P(("groups", "dp"), None, "tp"),
        P(("groups", "dp"), None, "tp"),
        P("groups", None),
        P("groups"),
        P(("groups", "dp"), None),
        P(("groups", "dp"), None, None, "tp"),
        P(("groups", "dp"), None, None, "tp"),
        P(("groups", "dp"), None, None, "tp"),
        P(("groups", "dp"), None, "tp"),
        P(("groups", "dp"), None, "tp"),
        P(("groups", "dp"), None, "tp"),
        P(("groups", "dp")),
    )
    out_specs = (P(("groups", "dp"), None, None, "tp"), P(("groups", "dp"), None, "tp"))
    return jax.shard_map(shards, mesh=mesh, in_specs=in_specs, out_specs=out_specs, check_vma=False)
```

```python
import functools

import jax
import jax.numpy as jnp
from jax import lax
from jax.experimental import pallas as pl
from jax.experimental.pallas import tpu as pltpu
from jax.sharding import PartitionSpec as P

HEAD = 128
LANES = 128
ROW_TILE = 16
MASKED = -1e30
RING_MAX = 16
VMEM_LIMIT = 40 * 1024 * 1024


def fill_pool(pieces, pool):
    row = 0
    for piece in pieces:
        pool[row : row + piece.shape[0]] = piece[...]
        row += piece.shape[0]


def blend(first, slot_ref, pool, placed, keep, blended):
    span_len = pool.shape[1]
    total = keep.shape[0]
    for j in range(total // span_len):
        at = slice(j * span_len, (j + 1) * span_len)
        kept = jnp.concatenate([keep[at, :]] * (blended.shape[1] // LANES), axis=1)
        blended[at, :] = placed[at, :] + kept * pool[slot_ref[first + j]]
    blended[total:, :] = placed[total:, :]


def prepare_kernel(
    count, place_ref, *rest
):
    sources, rest = rest[:12], rest[12:]
    scalars, limits, own_k, own_v, fk, fv, qk, qv, fq, qq, *rest = rest
    spans_ref, home_ref, sel_ref, length_ref, sems = rest
    req_count, picks, lists, width = fk.shape
    q_rows = qk.shape[1]
    spans_dev, span_len, _ = own_k.shape
    total = lists * span_len
    copies = [
        pltpu.make_async_copy(source, target, sems.at[n])
        for n, (source, target) in enumerate(
            zip(
                sources,
                (spans_ref, home_ref, sel_ref, length_ref, fk, fv, qk, qv, fq, qq, own_k, own_v),
                strict=True,
            )
        )
    ]
    for copy in copies:
        copy.start()
    lane = lax.broadcasted_iota(jnp.int32, (1, LANES), 1)
    asked_at = lane - picks * ROW_TILE
    blank = jnp.where((asked_at >= 0) & (asked_at < q_rows), total + asked_at, -1)
    for copy in copies[:4]:
        copy.wait()
    for r in range(req_count):
        limit = blank
        for j in range(lists):
            position = home_ref[spans_ref[r, j]]
            owner = lax.div(position, spans_dev)
            half = lax.div(owner, 2)
            place = jnp.where(lax.rem(owner, 2) == 0, half, count - 1 - half)
            upstream = lax.rem(place_ref[0] - place + count, count)
            scalars[r * lists + j] = upstream * spans_dev + lax.rem(position, spans_dev)
            for i in range(picks):
                limit = jnp.where(lane == i * ROW_TILE + j, j * span_len + sel_ref[i, position], limit)
        limits[r] = limit
        scalars[req_count * lists + r] = length_ref[r]
    for copy in copies[4:]:
        copy.wait()


def place_kernel(limits, fk, fv, qk, qv, placed, keep, bias, rows):
    req_count, picks, lists, width = fk.shape
    q_rows = qk.shape[1]
    total = keep.shape[1]
    rows[...] = jnp.zeros_like(rows)
    key = lax.broadcasted_iota(jnp.int32, (placed.shape[1], LANES), 0)
    for r in range(req_count):
        limit = limits[r]
        rows[0:picks, 0:lists, 0:width] = fk[r]
        rows[0:picks, 0:lists, width:] = fv[r]
        rows[picks : picks + q_rows // ROW_TILE, :, 0:width] = qk[r].reshape(-1, ROW_TILE, width)
        rows[picks : picks + q_rows // ROW_TILE, :, width:] = qv[r].reshape(-1, ROW_TILE, width)
        here = jnp.where(key == limit, 1.0, 0.0)
        placed[r] = jnp.dot(
            here.astype(jnp.bfloat16),
            rows[...].reshape(LANES, -1),
            preferred_element_type=jnp.float32,
        ).astype(jnp.bfloat16)
        taken = jnp.max(here[:total], axis=1, keepdims=True)
        keep[r] = jnp.broadcast_to(1.0 - taken, (total, LANES)).astype(jnp.bfloat16)
        bias[r] = jnp.where(key <= limit, 0.0, MASKED).astype(jnp.bfloat16)


def weights_kernel(n_buf, slot_ref, placed, keep, bias, fq, qq, *rest):
    pieces = rest[:n_buf]
    out_ref, pool, blended, units, queries = rest[n_buf:]
    req_count, picks, lists, _ = fq.shape
    kv_heads, heads, tiles = queries.shape[:3]
    rows_head = tiles * ROW_TILE
    width = blended.shape[1]
    row = lax.broadcasted_iota(jnp.int32, (rows_head, LANES), 0)
    column = lax.broadcasted_iota(jnp.int32, (rows_head, LANES), 1)
    unit = jnp.where(row == column, 1.0, 0.0).astype(jnp.bfloat16)
    for h in range(heads):
        units[h * rows_head : (h + 1) * rows_head, :] = unit
    fill_pool(pieces, pool)
    scale = 1.4426950408889634 / float(HEAD) ** 0.5
    for r in range(req_count):
        blend(r * lists, slot_ref, pool, placed.at[r, :, 0:width], keep.at[r], blended)
        for g in range(kv_heads):
            table = jnp.concatenate([blended[:, g * HEAD : (g + 1) * HEAD], bias[r]], axis=1)
            for h in range(heads):
                at = (g * heads + h) * HEAD
                queries[g, h, 0:picks, 0:lists, :] = fq[r, :, :, at : at + HEAD]
                queries[g, h, picks:, :, :] = qq[r, :, at : at + HEAD].reshape(-1, ROW_TILE, HEAD)
            stacked = queries[g].reshape(heads * rows_head, HEAD)
            scores = lax.dot_general(
                jnp.concatenate([stacked, units[...]], axis=1),
                table,
                (((1,), (1,)), ((), ())),
                preferred_element_type=jnp.float32,
            )
            top = jnp.max(scores, axis=1, keepdims=True)
            out_ref[r, g] = jnp.exp2((scores - top) * scale).astype(jnp.bfloat16)


def values_kernel(n_buf, slot_ref, w_ref, placed, keep, *rest):
    pieces = rest[:n_buf]
    redone_hbm, spoken_hbm, redone, spoken, pool, blended, out_sems = rest[n_buf:]
    req_count, picks, lists, _ = redone.shape
    kv_heads = w_ref.shape[1]
    q_rows = spoken.shape[1]
    heads = spoken.shape[2] // HEAD // kv_heads
    rows_head = picks * ROW_TILE + q_rows
    width = blended.shape[1]
    fill_pool(pieces, pool)

    def out_copies(r):
        return [
            pltpu.make_async_copy(redone.at[r], redone_hbm.at[r], out_sems.at[2 * r]),
            pltpu.make_async_copy(spoken.at[r], spoken_hbm.at[r], out_sems.at[2 * r + 1]),
        ]

    for r in range(req_count):
        blend(r * lists, slot_ref, pool, placed.at[r, :, width : 2 * width], keep.at[r], blended)
        ones = jnp.ones((blended.shape[0], LANES), jnp.bfloat16)
        length = slot_ref[req_count * lists + r]
        live = lax.broadcasted_iota(jnp.int32, (q_rows, HEAD), 0) < length
        for g in range(kv_heads):
            table = jnp.concatenate([blended[:, g * HEAD : (g + 1) * HEAD], ones], axis=1)
            both = jnp.dot(w_ref[r, g], table, preferred_element_type=jnp.float32)
            result = both[:, :HEAD] / both[:, HEAD:]
            for h in range(heads):
                at = (g * heads + h) * HEAD
                row = h * rows_head
                fresh = result[row : row + picks * ROW_TILE].astype(jnp.bfloat16)
                redone[r, :, :, at : at + HEAD] = fresh.reshape(picks, ROW_TILE, HEAD)[:, :lists, :]
                asked = result[row + picks * ROW_TILE : row + rows_head]
                spoken[r, :, at : at + HEAD] = jnp.where(live, asked, 0.0).astype(jnp.bfloat16)
        for copy in out_copies(r):
            copy.start()
    for r in range(req_count):
        for copy in out_copies(r):
            copy.wait()


SMEM_SPEC = pl.BlockSpec(memory_space=pltpu.SMEM)
VMEM_SPEC = pl.BlockSpec(memory_space=pltpu.VMEM)
HBM_SPEC = pl.BlockSpec(memory_space=pltpu.HBM)
PARAMS = pltpu.CompilerParams(vmem_limit_bytes=VMEM_LIMIT)


def in_vmem(x):
    return pltpu.with_memory_space_constraint(x, pltpu.VMEM)


def in_hbm(x):
    return pltpu.with_memory_space_constraint(x, pltpu.HBM)


def like(x):
    return pltpu.VMEM(x.shape, x.dtype)


def prepare(place, spans, home, sel, lengths, cache_k, cache_v, fresh_q, fresh_k, fresh_v, question_q, question_k, question_v):
    count = lax.axis_size("dp")
    req_count, picks, lists, _ = fresh_q.shape
    _, span_len, width = cache_k.shape
    q_rows = question_q.shape[1]
    total = lists * span_len
    padded = -(-(total + q_rows) // LANES) * LANES
    near = (spans, home, sel, lengths)
    held = (fresh_k, fresh_v, question_k, question_v, fresh_q, question_q)
    far = near + held + (cache_k, cache_v)
    bf16 = jnp.bfloat16
    scalars, limits, own_k, own_v, *held = pl.pallas_call(
        functools.partial(prepare_kernel, count),
        in_specs=[SMEM_SPEC] + [HBM_SPEC] * len(far),
        out_specs=[SMEM_SPEC] + [VMEM_SPEC] * (3 + len(held)),
        out_shape=[
            pltpu.SMEM((req_count * lists + req_count,), jnp.int32),
            pltpu.VMEM((req_count, 1, LANES), jnp.int32),
            like(cache_k),
            like(cache_v),
        ]
        + [like(x) for x in held],
        scratch_shapes=[pltpu.SMEM(x.shape, x.dtype) for x in near] + [pltpu.SemaphoreType.DMA((len(far),))],
        compiler_params=PARAMS,
        cost_estimate=pl.CostEstimate(flops=0, bytes_accessed=6 << 20, transcendentals=0),
        name="span_prepare",
    )(place, *map(in_hbm, far))
    placed, keep, bias = pl.pallas_call(
        place_kernel,
        in_specs=[VMEM_SPEC] * 5,
        out_specs=[VMEM_SPEC] * 3,
        out_shape=[
            pltpu.VMEM((req_count, padded, 2 * width), bf16),
            pltpu.VMEM((req_count, total, LANES), bf16),
            pltpu.VMEM((req_count, padded, LANES), bf16),
        ],
        scratch_shapes=[pltpu.VMEM((LANES // ROW_TILE, ROW_TILE, 2 * width), bf16)],
        compiler_params=PARAMS,
        cost_estimate=pl.CostEstimate(flops=0, bytes_accessed=3 << 20, transcendentals=0),
        name="span_place",
    )(*map(in_vmem, (limits, *held[:4])))
    return scalars, own_k, own_v, placed, keep, bias, held[4], held[5]


def attend(scalars, placed, keep, bias, fresh_q, question_q, k_pieces, v_pieces):
    req_count, picks, _, q_width = fresh_q.shape
    _, span_len, width = k_pieces[0].shape
    n_buf = len(k_pieces)
    kv_heads, heads = width // HEAD, q_width // width
    tiles = picks + question_q.shape[1] // ROW_TILE
    padded = placed.shape[1]
    pool = pltpu.VMEM((sum(x.shape[0] for x in k_pieces), span_len, width), jnp.bfloat16)
    blended = pltpu.VMEM((padded, width), jnp.bfloat16)
    w_shape = (req_count, kv_heads, heads * tiles * ROW_TILE, padded)
    flops = 4 * req_count * kv_heads * heads * tiles * ROW_TILE * padded * HEAD
    weights = pl.pallas_call(
        functools.partial(weights_kernel, n_buf),
        in_specs=[SMEM_SPEC] + [VMEM_SPEC] * (5 + n_buf),
        out_specs=VMEM_SPEC,
        scratch_shapes=[pool, blended, pltpu.VMEM((heads * tiles * ROW_TILE, LANES), jnp.bfloat16)]
        + [pltpu.VMEM((kv_heads, heads, tiles, ROW_TILE, HEAD), jnp.bfloat16)],
        out_shape=pltpu.VMEM(w_shape, jnp.bfloat16),
        compiler_params=PARAMS,
        cost_estimate=pl.CostEstimate(flops=flops, bytes_accessed=8 << 20, transcendentals=flops // 512),
        name="span_weights",
    )(scalars, *map(in_vmem, (placed, keep, bias, fresh_q, question_q)), *map(in_vmem, k_pieces))
    n_buf = len(v_pieces)
    return pl.pallas_call(
        functools.partial(values_kernel, n_buf),
        in_specs=[SMEM_SPEC] + [VMEM_SPEC] * (3 + n_buf),
        out_specs=[HBM_SPEC, HBM_SPEC],
        scratch_shapes=[
            like(fresh_q),
            like(question_q),
            pool,
            blended,
            pltpu.SemaphoreType.DMA((2 * req_count,)),
        ],
        out_shape=[
            jax.ShapeDtypeStruct(fresh_q.shape, jnp.bfloat16),
            jax.ShapeDtypeStruct(question_q.shape, jnp.bfloat16),
        ],
        compiler_params=PARAMS,
        cost_estimate=pl.CostEstimate(flops=flops, bytes_accessed=8 << 20, transcendentals=0),
        name="span_values",
    )(scalars, *map(in_vmem, (weights, placed, keep)), *map(in_vmem, v_pieces))


def ring_gather(keys, values, count, ready, later):
    order = list(range(0, count, 2)) + list(range(1, count, 2))[::-1]
    onward = [(order[i], order[(i + 1) % count]) for i in range(count)]
    back = [(b, a) for a, b in onward]
    half, rest = count // 2, (count - 1) // 2
    cut = keys.shape[0] // 2
    k_at, v_at = {0: [keys]}, {0: [values]}
    k_on = k_back = keys
    v_on = v_back = values
    for hop in range(1, rest + 1):
        k_on = lax.ppermute(k_on, "dp", onward)
        k_at[hop] = [k_on]
        k_back = lax.ppermute(k_back, "dp", back)
        k_at[count - hop] = [k_back]
        if hop == 2:
            k_back, _ = lax.optimization_barrier((k_back, later))
        if hop == 1:
            k_back, _ = lax.optimization_barrier((k_back, ready))
        v_on = lax.ppermute(v_on, "dp", onward)
        v_at[hop] = [v_on]
        v_back = lax.ppermute(v_back, "dp", back)
        v_at[count - hop] = [v_back]
    if half > rest:
        k_at[half] = [lax.ppermute(k_on, "dp", onward)]
        v_at[half] = [lax.ppermute(v_back, "dp", back)]
    gathered = []
    for at in (k_at, v_at):
        gathered.append([piece for d in range(count) for piece in at[d]])
    return gathered


def asked_gather(keys, values, positions, spans_dev, count):
    slot_count = positions.shape[0]
    capacity = (slot_count + count - 1) // count
    owner = positions // spans_dev
    local = positions % spans_dev
    ids = jnp.arange(slot_count, dtype=jnp.int32)
    earlier = (owner[:, None] == owner[None, :]) & (ids[None, :] < ids[:, None])
    slots = owner * capacity + jnp.sum(earlier.astype(jnp.int32), axis=1)
    asking = jnp.full((count * capacity,), -1, jnp.int32).at[slots].set(local)
    wanted = jnp.maximum(lax.all_to_all(asking, "dp", split_axis=0, concat_axis=0, tiled=True), 0)
    pieces = [
        [lax.all_to_all(cache[wanted], "dp", split_axis=0, concat_axis=0, tiled=True)]
        for cache in (keys, values)
    ]
    return slots, pieces[0], pieces[1]


def shards(
    cache_k,
    cache_v,
    sel_rows,
    span_home,
    request_spans,
    fresh_q,
    fresh_k,
    fresh_v,
    question_q,
    question_k,
    question_v,
    question_len,
):
    count = lax.axis_size("dp")
    spans_dev = cache_k.shape[0]
    turned_q, turned_k, turned_v = [jnp.transpose(x, (0, 2, 1, 3)) for x in (fresh_q, fresh_k, fresh_v)]
    me = lax.axis_index("dp")
    place = jnp.where(me % 2 == 0, me // 2, count - 1 - me // 2).astype(jnp.int32).reshape(1)
    scalars, own_k, own_v, placed, keep, bias, held_q, asked_q = prepare(
        place,
        request_spans,
        span_home,
        sel_rows.T,
        question_len,
        cache_k,
        cache_v,
        turned_q,
        turned_k,
        turned_v,
        question_q,
        question_k,
        question_v,
    )
    if count <= RING_MAX:
        k_pieces, v_pieces = ring_gather(cache_k, cache_v, count, own_k, bias)
        k_pieces[0], v_pieces[0] = own_k, own_v
        scalars = pltpu.with_memory_space_constraint(scalars, pltpu.SMEM)
    else:
        pool_ids = jnp.arange(span_home.shape[0], dtype=jnp.int32)
        named = request_spans.reshape(-1, 1) == pool_ids
        positions = jnp.sum(jnp.where(named, span_home, 0), axis=-1, dtype=jnp.int32)
        slots, k_pieces, v_pieces = asked_gather(cache_k, cache_v, positions, spans_dev, count)
        scalars = jnp.concatenate([slots, question_len])
    redone, spoken = attend(
        scalars, placed, keep, bias, held_q, asked_q, k_pieces, v_pieces
    )
    return jnp.transpose(redone, (0, 2, 1, 3)), spoken


def solution(mesh):
    in_specs = (
        P(("groups", "dp"), None, "tp"),
        P(("groups", "dp"), None, "tp"),
        P("groups", None),
        P("groups"),
        P(("groups", "dp"), None),
        P(("groups", "dp"), None, None, "tp"),
        P(("groups", "dp"), None, None, "tp"),
        P(("groups", "dp"), None, None, "tp"),
        P(("groups", "dp"), None, "tp"),
        P(("groups", "dp"), None, "tp"),
        P(("groups", "dp"), None, "tp"),
        P(("groups", "dp")),
    )
    out_specs = (P(("groups", "dp"), None, None, "tp"), P(("groups", "dp"), None, "tp"))
    return jax.shard_map(shards, mesh=mesh, in_specs=in_specs, out_specs=out_specs, check_vma=False)
```

```python
import functools

import jax
import jax.numpy as jnp
from jax import lax
from jax.experimental import pallas as pl
from jax.experimental.pallas import tpu as pltpu
from jax.sharding import PartitionSpec as P

HEAD = 128
LANES = 128
ROW_TILE = 16
MASKED = -1e30
RING_MAX = 16
VMEM_LIMIT = 40 * 1024 * 1024


def fill_pool(pieces, pool):
    row = 0
    for piece in pieces:
        pool[row : row + piece.shape[0]] = piece[...]
        row += piece.shape[0]


def blend(first, slot_ref, pool, placed, keep, blended):
    span_len = pool.shape[1]
    total = keep.shape[0]
    for j in range(total // span_len):
        at = slice(j * span_len, (j + 1) * span_len)
        kept = jnp.concatenate([keep[at, :]] * (blended.shape[1] // LANES), axis=1)
        blended[at, :] = placed[at, :] + kept * pool[slot_ref[first + j]]
    blended[total:, :] = placed[total:, :]


def prepare_kernel(
    count, place_ref, *rest
):
    sources, rest = rest[:12], rest[12:]
    scalars, limits, own_k, own_v, fk, fv, qk, qv, fq, qq, *rest = rest
    spans_ref, home_ref, sel_ref, length_ref, sems = rest
    req_count, picks, lists, width = fk.shape
    q_rows = qk.shape[1]
    spans_dev, span_len, _ = own_k.shape
    total = lists * span_len
    copies = [
        pltpu.make_async_copy(source, target, sems.at[n])
        for n, (source, target) in enumerate(
            zip(
                sources,
                (spans_ref, home_ref, sel_ref, length_ref, fk, fv, qk, qv, fq, qq, own_k, own_v),
                strict=True,
            )
        )
    ]
    for copy in copies:
        copy.start()
    lane = lax.broadcasted_iota(jnp.int32, (1, LANES), 1)
    asked_at = lane - picks * ROW_TILE
    blank = jnp.where((asked_at >= 0) & (asked_at < q_rows), total + asked_at, -1)
    for copy in copies[:4]:
        copy.wait()
    for r in range(req_count):
        limit = blank
        for j in range(lists):
            position = home_ref[spans_ref[r, j]]
            owner = lax.div(position, spans_dev)
            half = lax.div(owner, 2)
            place = jnp.where(lax.rem(owner, 2) == 0, half, count - 1 - half)
            upstream = lax.rem(place_ref[0] - place + count, count)
            scalars[r * lists + j] = upstream * spans_dev + lax.rem(position, spans_dev)
            for i in range(picks):
                limit = jnp.where(lane == i * ROW_TILE + j, j * span_len + sel_ref[i, position], limit)
        limits[r] = limit
        scalars[req_count * lists + r] = length_ref[r]
    for copy in copies[4:]:
        copy.wait()


def place_kernel(limits, fk, fv, qk, qv, fq, qq, placed, keep, bias, queries, rows):
    req_count, picks, lists, width = fk.shape
    q_rows = qk.shape[1]
    total = keep.shape[1]
    rows[...] = jnp.zeros_like(rows)
    key = lax.broadcasted_iota(jnp.int32, (placed.shape[1], LANES), 0)
    for r in range(req_count):
        limit = limits[r]
        rows[0:picks, 0:lists, 0:width] = fk[r]
        rows[0:picks, 0:lists, width:] = fv[r]
        rows[picks : picks + q_rows // ROW_TILE, :, 0:width] = qk[r].reshape(-1, ROW_TILE, width)
        rows[picks : picks + q_rows // ROW_TILE, :, width:] = qv[r].reshape(-1, ROW_TILE, width)
        here = jnp.where(key == limit, 1.0, 0.0)
        placed[r] = jnp.dot(
            here.astype(jnp.bfloat16),
            rows[...].reshape(LANES, -1),
            preferred_element_type=jnp.float32,
        ).astype(jnp.bfloat16)
        taken = jnp.max(here[:total], axis=1, keepdims=True)
        keep[r] = jnp.broadcast_to(1.0 - taken, (total, LANES)).astype(jnp.bfloat16)
        bias[r] = jnp.where(key <= limit, 0.0, MASKED).astype(jnp.bfloat16)
        for g in range(queries.shape[1]):
            for h in range(queries.shape[2]):
                at = (g * queries.shape[2] + h) * HEAD
                queries[r, g, h, 0:picks, 0:lists, :] = fq[r, :, :, at : at + HEAD]
                queries[r, g, h, picks:, :, :] = qq[r, :, at : at + HEAD].reshape(-1, ROW_TILE, HEAD)


def weights_kernel(n_buf, lists, slot_ref, placed, keep, bias, queries, *rest):
    pieces = rest[:n_buf]
    out_ref, pool, blended, units = rest[n_buf:]
    req_count, kv_heads, heads, tiles = queries.shape[:4]
    rows_head = tiles * ROW_TILE
    width = blended.shape[1]
    row = lax.broadcasted_iota(jnp.int32, (rows_head, LANES), 0)
    column = lax.broadcasted_iota(jnp.int32, (rows_head, LANES), 1)
    unit = jnp.where(row == column, 1.0, 0.0).astype(jnp.bfloat16)
    for h in range(heads):
        units[h * rows_head : (h + 1) * rows_head, :] = unit
    fill_pool(pieces, pool)
    scale = 1.4426950408889634 / float(HEAD) ** 0.5
    for r in range(req_count):
        blend(r * lists, slot_ref, pool, placed.at[r, :, 0:width], keep.at[r], blended)
        for g in range(kv_heads):
            table = jnp.concatenate([blended[:, g * HEAD : (g + 1) * HEAD], bias[r]], axis=1)
            stacked = queries[r, g].reshape(heads * rows_head, HEAD)
            scores = lax.dot_general(
                jnp.concatenate([stacked, units[...]], axis=1),
                table,
                (((1,), (1,)), ((), ())),
                preferred_element_type=jnp.float32,
            )
            top = jnp.max(scores, axis=1, keepdims=True)
            out_ref[r, g] = jnp.exp2((scores - top) * scale).astype(jnp.bfloat16)


def values_kernel(n_buf, slot_ref, w_ref, placed, keep, *rest):
    pieces = rest[:n_buf]
    redone_hbm, spoken_hbm, redone, spoken, pool, blended, out_sems = rest[n_buf:]
    req_count, picks, lists, _ = redone.shape
    kv_heads = w_ref.shape[1]
    q_rows = spoken.shape[1]
    heads = spoken.shape[2] // HEAD // kv_heads
    rows_head = picks * ROW_TILE + q_rows
    width = blended.shape[1]
    fill_pool(pieces, pool)

    def out_copies(r):
        return [
            pltpu.make_async_copy(redone.at[r], redone_hbm.at[r], out_sems.at[2 * r]),
            pltpu.make_async_copy(spoken.at[r], spoken_hbm.at[r], out_sems.at[2 * r + 1]),
        ]

    for r in range(req_count):
        blend(r * lists, slot_ref, pool, placed.at[r, :, width : 2 * width], keep.at[r], blended)
        ones = jnp.ones((blended.shape[0], LANES), jnp.bfloat16)
        length = slot_ref[req_count * lists + r]
        live = lax.broadcasted_iota(jnp.int32, (q_rows, HEAD), 0) < length
        for g in range(kv_heads):
            table = jnp.concatenate([blended[:, g * HEAD : (g + 1) * HEAD], ones], axis=1)
            both = jnp.dot(w_ref[r, g], table, preferred_element_type=jnp.float32)
            result = both[:, :HEAD] / both[:, HEAD:]
            for h in range(heads):
                at = (g * heads + h) * HEAD
                row = h * rows_head
                fresh = result[row : row + picks * ROW_TILE].astype(jnp.bfloat16)
                redone[r, :, :, at : at + HEAD] = fresh.reshape(picks, ROW_TILE, HEAD)[:, :lists, :]
                asked = result[row + picks * ROW_TILE : row + rows_head]
                spoken[r, :, at : at + HEAD] = jnp.where(live, asked, 0.0).astype(jnp.bfloat16)
        for copy in out_copies(r):
            copy.start()
    for r in range(req_count):
        for copy in out_copies(r):
            copy.wait()


SMEM_SPEC = pl.BlockSpec(memory_space=pltpu.SMEM)
VMEM_SPEC = pl.BlockSpec(memory_space=pltpu.VMEM)
HBM_SPEC = pl.BlockSpec(memory_space=pltpu.HBM)
PARAMS = pltpu.CompilerParams(vmem_limit_bytes=VMEM_LIMIT)


def in_vmem(x):
    return pltpu.with_memory_space_constraint(x, pltpu.VMEM)


def in_hbm(x):
    return pltpu.with_memory_space_constraint(x, pltpu.HBM)


def like(x):
    return pltpu.VMEM(x.shape, x.dtype)


def prepare(place, spans, home, sel, lengths, cache_k, cache_v, fresh_q, fresh_k, fresh_v, question_q, question_k, question_v):
    count = lax.axis_size("dp")
    req_count, picks, lists, q_width = fresh_q.shape
    _, span_len, width = cache_k.shape
    q_rows = question_q.shape[1]
    kv_heads, heads = width // HEAD, q_width // width
    total = lists * span_len
    padded = -(-(total + q_rows) // LANES) * LANES
    near = (spans, home, sel, lengths)
    held = (fresh_k, fresh_v, question_k, question_v, fresh_q, question_q)
    far = near + held + (cache_k, cache_v)
    bf16 = jnp.bfloat16
    scalars, limits, own_k, own_v, *held = pl.pallas_call(
        functools.partial(prepare_kernel, count),
        in_specs=[SMEM_SPEC] + [HBM_SPEC] * len(far),
        out_specs=[SMEM_SPEC] + [VMEM_SPEC] * (3 + len(held)),
        out_shape=[
            pltpu.SMEM((req_count * lists + req_count,), jnp.int32),
            pltpu.VMEM((req_count, 1, LANES), jnp.int32),
            like(cache_k),
            like(cache_v),
        ]
        + [like(x) for x in held],
        scratch_shapes=[pltpu.SMEM(x.shape, x.dtype) for x in near] + [pltpu.SemaphoreType.DMA((len(far),))],
        compiler_params=PARAMS,
        cost_estimate=pl.CostEstimate(flops=0, bytes_accessed=6 << 20, transcendentals=0),
        name="span_prepare",
    )(place, *map(in_hbm, far))
    placed, keep, bias, queries = pl.pallas_call(
        place_kernel,
        in_specs=[VMEM_SPEC] * 7,
        out_specs=[VMEM_SPEC] * 4,
        out_shape=[
            pltpu.VMEM((req_count, padded, 2 * width), bf16),
            pltpu.VMEM((req_count, total, LANES), bf16),
            pltpu.VMEM((req_count, padded, LANES), bf16),
            pltpu.VMEM((req_count, kv_heads, heads, picks + q_rows // ROW_TILE, ROW_TILE, HEAD), bf16),
        ],
        scratch_shapes=[pltpu.VMEM((LANES // ROW_TILE, ROW_TILE, 2 * width), bf16)],
        compiler_params=PARAMS,
        cost_estimate=pl.CostEstimate(flops=0, bytes_accessed=3 << 20, transcendentals=0),
        name="span_place",
    )(*map(in_vmem, (limits, *held)))
    return scalars, own_k, own_v, placed, keep, bias, queries


def attend(scalars, placed, keep, bias, queries, fresh_q, question_q, k_pieces, v_pieces):
    req_count, _, lists, _ = fresh_q.shape
    _, span_len, width = k_pieces[0].shape
    n_buf = len(k_pieces)
    kv_heads, heads, tiles = queries.shape[1:4]
    padded = placed.shape[1]
    pool = pltpu.VMEM((sum(x.shape[0] for x in k_pieces), span_len, width), jnp.bfloat16)
    blended = pltpu.VMEM((padded, width), jnp.bfloat16)
    w_shape = (req_count, kv_heads, heads * tiles * ROW_TILE, padded)
    flops = 4 * req_count * kv_heads * heads * tiles * ROW_TILE * padded * HEAD
    weights = pl.pallas_call(
        functools.partial(weights_kernel, n_buf, lists),
        in_specs=[SMEM_SPEC] + [VMEM_SPEC] * (4 + n_buf),
        out_specs=VMEM_SPEC,
        scratch_shapes=[pool, blended, pltpu.VMEM((heads * tiles * ROW_TILE, LANES), jnp.bfloat16)],
        out_shape=pltpu.VMEM(w_shape, jnp.bfloat16),
        compiler_params=PARAMS,
        cost_estimate=pl.CostEstimate(flops=flops, bytes_accessed=8 << 20, transcendentals=flops // 512),
        name="span_weights",
    )(scalars, *map(in_vmem, (placed, keep, bias, queries)), *map(in_vmem, k_pieces))
    n_buf = len(v_pieces)
    return pl.pallas_call(
        functools.partial(values_kernel, n_buf),
        in_specs=[SMEM_SPEC] + [VMEM_SPEC] * (3 + n_buf),
        out_specs=[HBM_SPEC, HBM_SPEC],
        scratch_shapes=[
            like(fresh_q),
            like(question_q),
            pool,
            blended,
            pltpu.SemaphoreType.DMA((2 * req_count,)),
        ],
        out_shape=[
            jax.ShapeDtypeStruct(fresh_q.shape, jnp.bfloat16),
            jax.ShapeDtypeStruct(question_q.shape, jnp.bfloat16),
        ],
        compiler_params=PARAMS,
        cost_estimate=pl.CostEstimate(flops=flops, bytes_accessed=8 << 20, transcendentals=0),
        name="span_values",
    )(scalars, *map(in_vmem, (weights, placed, keep)), *map(in_vmem, v_pieces))


def ring_gather(keys, values, count, ready, later):
    order = list(range(0, count, 2)) + list(range(1, count, 2))[::-1]
    onward = [(order[i], order[(i + 1) % count]) for i in range(count)]
    back = [(b, a) for a, b in onward]
    half, rest = count // 2, (count - 1) // 2
    cut = keys.shape[0] // 2
    k_at, v_at = {0: [keys]}, {0: [values]}
    k_on = k_back = keys
    v_on = v_back = values
    for hop in range(1, rest + 1):
        k_on = lax.ppermute(k_on, "dp", onward)
        k_at[hop] = [k_on]
        k_back = lax.ppermute(k_back, "dp", back)
        k_at[count - hop] = [k_back]
        if hop == 2:
            k_back, _ = lax.optimization_barrier((k_back, later))
        if hop == 1:
            k_back, _ = lax.optimization_barrier((k_back, ready))
        v_on = lax.ppermute(v_on, "dp", onward)
        v_at[hop] = [v_on]
        v_back = lax.ppermute(v_back, "dp", back)
        v_at[count - hop] = [v_back]
    if half > rest:
        k_at[half] = [lax.ppermute(k_on, "dp", onward)]
        v_at[half] = [lax.ppermute(v_back, "dp", back)]
    gathered = []
    for at in (k_at, v_at):
        gathered.append([piece for d in range(count) for piece in at[d]])
    return gathered


def asked_gather(keys, values, positions, spans_dev, count):
    slot_count = positions.shape[0]
    capacity = (slot_count + count - 1) // count
    owner = positions // spans_dev
    local = positions % spans_dev
    ids = jnp.arange(slot_count, dtype=jnp.int32)
    earlier = (owner[:, None] == owner[None, :]) & (ids[None, :] < ids[:, None])
    slots = owner * capacity + jnp.sum(earlier.astype(jnp.int32), axis=1)
    asking = jnp.full((count * capacity,), -1, jnp.int32).at[slots].set(local)
    wanted = jnp.maximum(lax.all_to_all(asking, "dp", split_axis=0, concat_axis=0, tiled=True), 0)
    pieces = [
        [lax.all_to_all(cache[wanted], "dp", split_axis=0, concat_axis=0, tiled=True)]
        for cache in (keys, values)
    ]
    return slots, pieces[0], pieces[1]


def shards(
    cache_k,
    cache_v,
    sel_rows,
    span_home,
    request_spans,
    fresh_q,
    fresh_k,
    fresh_v,
    question_q,
    question_k,
    question_v,
    question_len,
):
    count = lax.axis_size("dp")
    spans_dev = cache_k.shape[0]
    turned_q, turned_k, turned_v = [jnp.transpose(x, (0, 2, 1, 3)) for x in (fresh_q, fresh_k, fresh_v)]
    me = lax.axis_index("dp")
    place = jnp.where(me % 2 == 0, me // 2, count - 1 - me // 2).astype(jnp.int32).reshape(1)
    scalars, own_k, own_v, placed, keep, bias, queries = prepare(
        place,
        request_spans,
        span_home,
        sel_rows.T,
        question_len,
        cache_k,
        cache_v,
        turned_q,
        turned_k,
        turned_v,
        question_q,
        question_k,
        question_v,
    )
    if count <= RING_MAX:
        k_pieces, v_pieces = ring_gather(cache_k, cache_v, count, own_k, bias)
        k_pieces[0], v_pieces[0] = own_k, own_v
        scalars = pltpu.with_memory_space_constraint(scalars, pltpu.SMEM)
    else:
        pool_ids = jnp.arange(span_home.shape[0], dtype=jnp.int32)
        named = request_spans.reshape(-1, 1) == pool_ids
        positions = jnp.sum(jnp.where(named, span_home, 0), axis=-1, dtype=jnp.int32)
        slots, k_pieces, v_pieces = asked_gather(cache_k, cache_v, positions, spans_dev, count)
        scalars = jnp.concatenate([slots, question_len])
    redone, spoken = attend(
        scalars, placed, keep, bias, queries, turned_q, question_q, k_pieces, v_pieces
    )
    return jnp.transpose(redone, (0, 2, 1, 3)), spoken


def solution(mesh):
    in_specs = (
        P(("groups", "dp"), None, "tp"),
        P(("groups", "dp"), None, "tp"),
        P("groups", None),
        P("groups"),
        P(("groups", "dp"), None),
        P(("groups", "dp"), None, None, "tp"),
        P(("groups", "dp"), None, None, "tp"),
        P(("groups", "dp"), None, None, "tp"),
        P(("groups", "dp"), None, "tp"),
        P(("groups", "dp"), None, "tp"),
        P(("groups", "dp"), None, "tp"),
        P(("groups", "dp")),
    )
    out_specs = (P(("groups", "dp"), None, None, "tp"), P(("groups", "dp"), None, "tp"))
    return jax.shard_map(shards, mesh=mesh, in_specs=in_specs, out_specs=out_specs, check_vma=False)
```
